256 devices in a mesh: row: 8 (over y_hi, x), col: 16 (over z, y_lo), sea: 2 (over core).
Axes of the slice: x: 4, y: 4 (y_hi: 2, y_lo: 2; y = y_hi * 2 + y_lo), z: 8, core: 2. Of those that a mesh axis runs over, the one named last changes fastest.
Arguments:
- kernel: bfloat16 [16, 8, 768, 6144], P(None, None, 'col', 'row'), may hold values from -0.01953125 to 0.01953125
- history: bfloat16 [15, 8, 768, 512], P(None, None, 'col', 'sea'), may hold values from -6 to 6
- displacement: float32 [6144, 512], P(('row', 'col'), 'sea'), may hold values from -6 to 6
- velocity: float32 [6144, 512], P(('row', 'col'), 'sea'), may hold values from -6 to 6
- acceleration: float32 [6144, 512], P(('row', 'col'), 'sea'), may hold values from -6 to 6
- excitation: float32 [3, 6144, 512], P(None, ('row', 'col'), 'sea'), may hold values from -6 to 6
- solve_inverse: float32 [1024, 6, 6], P(('row', 'col')), may hold values from -2.5 to 2.5
- stiffness: float32 [1024, 6, 6], P(('row', 'col')), may hold values from -2.5 to 2.5
- owned: int32 [1024], replicated, may hold values from 0 to 1023, as said below
- links: int32 [1024, 16], P(('row', 'col')), may hold values from 0 to 16383, as said below
- arms: float32 [1024, 3, 16], P(('row', 'col')), may hold values from -1 to 1
Outputs:
- final_velocity: float32 [6144, 512], P(('row', 'col'), 'sea')
- deck_gaps: float32 [1024, 16, 3, 512], P(('row', 'col'), None, None, 'sea')
The draws below stay inside these ranges and needn't reach their ends.
Inputs may be any that keep to these rules, and one draw needn't show every extreme that they name: `owned`: A permutation of the 1024 modules. Module m has its modes on the grid device m // 8 (row-major over row, col); its owner has the same col. The modules that one device sends to one owner number at most 2, exactly 2 wherever any are sent, and their list positions differ modulo 2. `links`: the partner point lies on another module listed to the same owner.
All inputs are finite; a program needn't handle non-finite values.
Results may differ from the reference program's by a relative error of at most 0.00037.
Values may be sent and summed in bfloat16 or wider, within the bound.
A program may use at most 128 MiB of HBM per device.

```python
import jax
import jax.numpy as jnp
from jax import lax

MOD_DEV = 8
MODULES = 1024
MODES = 6144
POINTS = 16
LAGS = 16
STEPS = 3
REALS = 512
BLOCK = 768
CAP = 2
N_ROW = 8
N_COL = 16


def ownership_tables(key):
    base_key = jax.random.fold_in(key, 11)
    col_keys = jax.random.split(base_key, N_COL)

    def one_column(col_key):
        order_key, offset_key = jax.random.split(col_key)
        row_order = jax.random.permutation(order_key, N_ROW)
        row_inverse = jnp.argsort(row_order)
        offsets = jax.random.permutation(offset_key, N_ROW)[:N_ROW // 2]
        slot_range = jnp.arange(MOD_DEV)
        return (row_inverse[:, None] - offsets[slot_range // CAP][None, :]) % N_ROW
    sources = jax.vmap(one_column)(col_keys)
    col_range = jnp.arange(N_COL)
    modules = (sources * N_COL + col_range[:, None, None]) * MOD_DEV + jnp.arange(MOD_DEV)[None, None, :]
    owner_list = jnp.transpose(modules, (1, 0, 2)).reshape(MODULES)
    link_key_a, link_key_b = jax.random.split(jax.random.fold_in(key, 23))
    steps_ahead = jax.random.randint(link_key_a, (MODULES, POINTS), 1, MOD_DEV)
    partner_points = jax.random.randint(link_key_b, (MODULES, POINTS), 0, POINTS)
    positions = jnp.arange(MODULES)[:, None]
    partner_modules = positions // MOD_DEV * MOD_DEV + (positions % MOD_DEV + steps_ahead) % MOD_DEV
    link_table = partner_modules * POINTS + partner_points
    return (owner_list.astype(jnp.int32), link_table.astype(jnp.int32))


def draw_owned(key, part):
    return ownership_tables(key)[0]


def draw_links(key, part):
    return ownership_tables(key)[1]


def block_scale(rng, dims, cuts, smallest, top_value):
    def one(dim, blocks):
        heights = jax.random.uniform(jax.random.fold_in(jax.random.fold_in(rng, 6), dim), (blocks,), jnp.float32, smallest / len(cuts), top_value / len(cuts))
        return jnp.repeat(jnp.exp(heights), dims[dim] // blocks).reshape((-1,) + (1,) * (len(dims) - dim - 1))

    factor_of = one(*cuts[0])
    for cut in cuts[1:]:
        factor_of = factor_of * one(*cut)
    return factor_of


def centred(own_key, shape, spread, most, cuts=(), kind=jnp.bfloat16):
    loudness = block_scale(own_key, shape, cuts, -0.22, 0.18) if cuts else 1.0
    array = jax.random.normal(own_key, shape, jnp.float32) * spread * loudness
    return jnp.minimum(jnp.maximum(array, -most), most).astype(kind)


def setup_inputs(seed: int = 0) -> dict:
    splits = jax.random.split(jax.random.key(seed), 12)
    kernel = centred(splits[0], (LAGS, N_ROW, BLOCK, MODES), (LAGS * MODES) ** -0.5, 0.01953125, ((2, 16), (3, 8)))
    history = centred(splits[1], (LAGS - 1, N_ROW, BLOCK, REALS), 1.0, 6.0, ((2, 16), (3, 2)))
    displacement = centred(splits[2], (MODES, REALS), 1.0, 6.0, ((0, 128), (1, 2)), jnp.float32)
    velocity = centred(splits[3], (MODES, REALS), 1.0, 6.0, ((0, 128), (1, 2)), jnp.float32)
    acceleration = centred(splits[4], (MODES, REALS), 1.0, 6.0, ((0, 128), (1, 2)), jnp.float32)
    excitation = centred(splits[5], (STEPS, MODES, REALS), 1.0, 6.0, ((1, 128), (2, 2)), jnp.float32)
    solve_inverse = centred(splits[6], (MODULES, 6, 6), 6 ** -0.5, 2.5, ((0, 128),), jnp.float32)
    stiffness = centred(splits[7], (MODULES, 6, 6), 6 ** -0.5, 2.5, ((0, 128),), jnp.float32)
    owned = draw_owned(jax.random.fold_in(splits[11], 71), 0)
    links = draw_links(jax.random.fold_in(splits[11], 71), 0)
    arms = jnp.clip(jax.random.uniform(splits[10], (MODULES, 3, POINTS), jnp.float32, -1.0, 1.0) * block_scale(splits[10], (MODULES, 3, POINTS), ((0, 128),), -0.4, 0.0), -1.0, 1.0)
    return dict(kernel=kernel, history=history, displacement=displacement, velocity=velocity, acceleration=acceleration, excitation=excitation, solve_inverse=solve_inverse, stiffness=stiffness, owned=owned, links=links, arms=arms)


DT = 0.5
QUARTER = DT * DT / 4.0


def blocks(matrix, vector):
    return jnp.einsum('mab,mbr->mar', matrix, vector, precision=lax.Precision.HIGHEST)


def newmark(displacement, velocity, acceleration, force_now, excitation_now, solve_inverse, stiffness):
    block_shape = (displacement.shape[0] // 6, 6, displacement.shape[1])
    predicted = displacement + DT * velocity + QUARTER * acceleration
    load_total = excitation_now - force_now - blocks(stiffness, predicted.reshape(block_shape)).reshape(displacement.shape)
    accel_next = blocks(solve_inverse, load_total.reshape(block_shape)).reshape(displacement.shape)
    return predicted + QUARTER * accel_next, velocity + 0.5 * DT * (acceleration + accel_next), accel_next


def deck_motion(motion, levers):
    moving = motion[:, 0:3, None, :]
    turning = motion[:, 3:6, None, :]
    arm_all = levers[:, :, :, None]
    surge_motion = moving[:, 0] + turning[:, 1] * arm_all[:, 2] - turning[:, 2] * arm_all[:, 1]
    sway_motion = moving[:, 1] + turning[:, 2] * arm_all[:, 0] - turning[:, 0] * arm_all[:, 2]
    heave_motion = moving[:, 2] + turning[:, 0] * arm_all[:, 1] - turning[:, 1] * arm_all[:, 0]
    return jnp.stack([surge_motion, sway_motion, heave_motion], axis=2)


def radiation(kernel, window):
    def add_lag(running, lag_pair):
        lag_kernel, lag_window = lag_pair
        flat_kernel = lag_kernel.reshape(MODES, MODES)
        flat_window = lag_window.reshape(MODES, REALS)
        return running + lax.dot_general(flat_kernel, flat_window, (((0,), (0,)), ((), ())), preferred_element_type=jnp.float32), None
    running, unused = lax.scan(add_lag, jnp.zeros((MODES, REALS), jnp.float32), (kernel, window))
    return running


def reference(kernel, history, displacement, velocity, acceleration, excitation, solve_inverse, stiffness, owned, links, arms):
    window = history
    for step_index in range(STEPS):
        newest = velocity.astype(jnp.bfloat16).reshape(1, N_ROW, BLOCK, REALS)
        window = jnp.concatenate([newest, window[:LAGS - 1]], axis=0)
        force_now = radiation(kernel, window)
        displacement, velocity, acceleration = newmark(displacement, velocity, acceleration, force_now, excitation[step_index], solve_inverse, stiffness)
    motion = displacement.reshape(MODULES, 6, REALS)
    owned_motion = jnp.take(motion, owned.astype(jnp.int32), axis=0)
    points = deck_motion(owned_motion, arms).reshape(MODULES * POINTS, 3, REALS)
    partner = jnp.take(points, links.reshape(-1).astype(jnp.int32), axis=0)
    deck_gaps = (points - partner).reshape(MODULES, POINTS, 3, REALS)
    return (velocity, deck_gaps)
```

```python
import functools

import jax
import jax.numpy as jnp
from jax import lax
from jax.experimental import pallas as pl
from jax.experimental.pallas import tpu as pltpu
from jax.sharding import PartitionSpec as P

POINTS = 16
STEPS = 3
SLOTS = 2
LANE_ROWS = 16

DT = 0.5
QUARTER = DT * DT / 4.0
MESH = pl.DeviceIdType.MESH
EXACT = lax.Precision.HIGHEST


def iota(shape, dim):
    return lax.broadcasted_iota(jnp.int32, shape, dim)


def f32(mask):
    return jnp.where(mask, 1.0, 0.0).astype(jnp.float32)


def dot(a, b, precision=None):
    return lax.dot_general(
        a, b, (((1,), (0,)), ((), ())), precision=precision, preferred_element_type=jnp.float32
    )


def dot_nt(a, b, precision=None):
    return lax.dot_general(
        a, b, (((1,), (1,)), ((), ())), precision=precision, preferred_element_type=jnp.float32
    )


def block_diagonal(ref, modules):
    size = 6 * modules
    rows = []
    for m in range(modules):
        place = f32(iota((6, size), 1) == iota((6, size), 0) + 6 * m)
        rows.append(dot(ref[m], place, EXACT))
    return jnp.concatenate(rows, axis=0)


def routing_matrix(owned, base, modules):
    n_row, lanes = owned.shape
    lane = iota((n_row, lanes), 1)
    column = iota((n_row, modules), 1)
    out_rows = n_row * LANE_ROWS
    spread = f32(iota((modules, 6 * modules), 1) // 6 == iota((modules, 6 * modules), 0))
    total = jnp.zeros((out_rows, 6 * modules), jnp.float32)
    for slot in range(SLOTS):
        hit = jnp.zeros((n_row, modules), jnp.float32)
        for m in range(modules):
            here = f32((owned == base + m) & (lane % SLOTS == slot))
            hit = jnp.where(column == m, jnp.sum(here, axis=1, keepdims=True), hit)
        r = iota((out_rows, n_row), 0)
        lift = f32(
            (r // LANE_ROWS == iota((out_rows, n_row), 1))
            & (r % LANE_ROWS >= 6 * slot)
            & (r % LANE_ROWS < 6 * slot + 6)
        )
        wide = dot(dot(lift, hit), spread)
        rr = iota((out_rows, 6 * modules), 0) % LANE_ROWS - 6 * slot
        total = total + jnp.where(rr == iota((out_rows, 6 * modules), 1) % 6, wide, 0.0)
    return total


def choice_matrix(owned, row, col, home_size, modules):
    n_row, lanes = owned.shape
    home = owned // home_size
    mine = jnp.sum(jnp.where(iota((n_row, lanes), 0) == row, home, 0), axis=0, keepdims=True)
    per_lane = f32(iota((n_row, lanes), 0) == mine)
    size = 6 * modules
    pick = f32(iota((size, lanes), 1) == col * modules + iota((size, lanes), 0) // 6)
    by_row = dot_nt(pick, per_lane)
    out = n_row * LANE_ROWS
    widen = f32(iota((n_row, out), 1) // LANE_ROWS == iota((n_row, out), 0))
    wide = dot(by_row, widen)
    i = iota((size, out), 0)
    fits = iota((size, out), 1) % LANE_ROWS == 6 * (i // 6 % SLOTS) + i % 6
    return jnp.where(fits, wide, 0.0)


def gap_matrix(links_ref, arms_ref, first_point, modules):
    rows, size = 3 * POINTS, 6 * modules
    by_point = f32(iota((rows, POINTS), 0) // 3 == iota((rows, POINTS), 1))
    levers = [dot_nt(by_point, arms_ref[t], EXACT) for t in range(modules)]
    lane = iota((rows, size), 1)
    comp = iota((rows, size), 0) % 3
    mode = lane % 6
    form = f32(mode == comp)
    for d in range(3):
        along = jnp.zeros((rows, size), jnp.float32)
        for t in range(modules):
            along = jnp.where(lane // 6 == t, levers[t][:, d : d + 1], along)
        plus = mode == 3 + (comp + 1) % 3
        minus = mode == 3 + (comp + 2) % 3
        form = form + jnp.where(plus & (d == (comp + 2) % 3), along, 0.0)
        form = form - jnp.where(minus & (d == (comp + 1) % 3), along, 0.0)
    local = (links_ref[...] - first_point).astype(jnp.float32)
    partner = dot_nt(by_point, local, EXACT).astype(jnp.int32)
    wide = iota((rows, rows), 1)
    out = []
    for t in range(modules):
        met = partner[:, t : t + 1]
        pick = f32((met % POINTS == wide // 3) & (wide % 3 == iota((rows, rows), 0) % 3))
        other = dot(pick, form, EXACT)
        out.append(
            jnp.where(lane // 6 == t, form, 0.0) - jnp.where(lane // 6 == met // POINTS, other, 0.0)
        )
    return jnp.concatenate(out, axis=0)


def steps_kernel(
    n_row, n_col, lags, groups,
    kernel_hbm, history_hbm, x_hbm, v_hbm, a_hbm, exc_hbm, solve_hbm, stiff_hbm, owned_hbm, links_hbm, arms_hbm,
    v_out, deck_out,
    kern, hist, hist_t, x, v, a, exc, solve, stiff, owned, links, arms,
    k_t, acc, base_force, force, newest, window, received, outgoing, arrived, gaps, routing,
    local_sem, ag_send, ag_recv, rs_send, rs_recv, ex_send, ex_recv,
):
    row, col = lax.axis_index("row"), lax.axis_index("col")
    slab, reals = v.shape
    modules = slab // 6
    depth = n_row * slab
    block = n_col * slab
    grid_index = row * n_col + col

    sems = iter(range(64))

    def fetch(src, dst):
        copy = pltpu.make_async_copy(src, dst, local_sem.at[next(sems)])
        copy.start()
        return copy

    get_v = fetch(v_hbm, v)
    get_first = fetch(kernel_hbm.at[pl.ds(0, 1)], kern.at[pl.ds(0, 1)])
    get_groups = []
    for first, last in groups:
        get_groups.append(
            (
                fetch(history_hbm.at[pl.ds(first - 1, last - first)], hist.at[pl.ds(first - 1, last - first)]),
                fetch(kernel_hbm.at[pl.ds(first, last - first)], kern.at[pl.ds(first, last - first)]),
            )
        )
    get_state = [fetch(x_hbm, x), fetch(a_hbm, a), fetch(exc_hbm, exc), fetch(solve_hbm, solve), fetch(stiff_hbm, stiff)]
    get_tables = [fetch(owned_hbm, owned), fetch(links_hbm, links), fetch(arms_hbm, arms)]

    row_peers = [lax.rem(row + d, n_row) for d in range(1, n_row)]
    col_peers = [lax.rem(col + d, n_col) for d in range(1, n_col)]
    barrier = pltpu.get_barrier_semaphore()
    for peer in row_peers:
        pl.semaphore_signal(barrier, inc=1, device_id={"row": peer}, device_id_type=MESH)
    for peer in col_peers:
        pl.semaphore_signal(barrier, inc=1, device_id={"col": peer}, device_id_type=MESH)
    pl.semaphore_wait(barrier, n_row + n_col - 2)

    def gather_copy(step, peer, source):
        return pltpu.make_async_remote_copy(
            src_ref=newest.at[step],
            dst_ref=window.at[step, source],
            send_sem=ag_send.at[step, peer],
            recv_sem=ag_recv.at[step, source],
            device_id={"row": peer},
            device_id_type=MESH,
        )

    def start_gather(step, value):
        newest[step] = value
        for peer in row_peers:
            gather_copy(step, peer, row).start()
        window[step, row] = value

    def wait_gather(step):
        for peer in row_peers:
            gather_copy(step, peer, peer).wait_recv()

    def scatter_copy(step, peer, source):
        return pltpu.make_async_remote_copy(
            src_ref=force.at[step, peer],
            dst_ref=received.at[step, source],
            send_sem=rs_send.at[step, peer],
            recv_sem=rs_recv.at[step, source],
            device_id={"col": peer},
            device_id_type=MESH,
        )

    def exchange_copy(peer, source):
        return pltpu.make_async_remote_copy(
            src_ref=outgoing.at[peer],
            dst_ref=arrived.at[source],
            send_sem=ex_send.at[peer],
            recv_sem=ex_recv.at[source],
            device_id={"row": peer},
            device_id_type=MESH,
        )

    def lag_block(k, count=1):
        return kern[pl.ds(k, count)].reshape(count * depth, block)

    def window_of(step):
        return window[step].reshape(depth, reals)

    def history_force(step, group_size, wait):
        acc[...] = jnp.zeros_like(acc)
        for index, (first, last) in enumerate(wait):
            if step == 0:
                for copy in get_groups[index]:
                    copy.wait()
                for k in range(first - 1, last - 1):
                    hist_t[:, k * depth : (k + 1) * depth] = hist[k].reshape(depth, reals).T
            low, high = first - 1 - step, last - 1 - step
            acc[...] += dot(hist_t[:, low * depth : high * depth], lag_block(first, last - first))
        base_force[step] = acc[...].T

    get_v.wait()
    start_gather(0, v[...].astype(jnp.bfloat16))
    get_first.wait()
    k_t[0] = lag_block(0).T
    history_force(0, None, groups)

    def send_force(step):
        wait_gather(step)
        force[step] = (base_force[step] + dot(k_t[0], window_of(step))).reshape(n_col, slab, reals)
        for peer in col_peers:
            scatter_copy(step, peer, col).start()

    send_force(0)

    for copy in get_state:
        copy.wait()
    solve_wide = block_diagonal(solve, modules)
    stiff_wide = block_diagonal(stiff, modules)

    displacement, velocity, acceleration = x[...], v[...], a[...]
    for step in range(STEPS):
        predicted = displacement + DT * velocity + QUARTER * acceleration
        known = dot(solve_wide, exc[step] - dot(stiff_wide, predicted, EXACT), EXACT)
        drift = velocity + 0.5 * DT * (acceleration + known)
        if step == 0:
            for later in (1, 2):
                k_t[later] = lag_block(later).T
            history_force(1, None, [(k, min(k + 2, lags)) for k in range(2, lags, 2)])
            base_force[1] = base_force[1] + dot(k_t[1], window_of(0))
            base_force[2] = dot(k_t[2], window_of(0))
        if step == 1:
            first_part = base_force[2]
            history_force(2, None, [(k, min(k + 2, lags)) for k in range(3, lags, 2)])
            base_force[2] = base_force[2] + first_part + dot(k_t[1], window_of(1))
        if step == 2:
            for copy in get_tables:
                copy.wait()
            routing[...] = routing_matrix(owned[...], grid_index * modules, modules)
            gaps[...] = dot(
                gap_matrix(links, arms, grid_index * modules * POINTS, modules),
                choice_matrix(owned[...], row, col, n_col * modules, modules),
                EXACT,
            )
        for peer in col_peers:
            scatter_copy(step, peer, peer).wait_recv()
        received[step, col] = force[step, col]
        total = received[step, 0]
        for source in range(1, n_col):
            total = total + received[step, source]
        answer = dot(solve_wide, total, EXACT)
        velocity = drift - 0.5 * DT * answer
        if step + 1 < STEPS:
            start_gather(step + 1, velocity.astype(jnp.bfloat16))
        acceleration = known - answer
        displacement = predicted + QUARTER * acceleration
        if step + 1 < STEPS:
            send_force(step + 1)

    outgoing[...] = dot(routing[...], displacement, EXACT).reshape(n_row, LANE_ROWS, reals)
    for peer in row_peers:
        exchange_copy(peer, row).start()
    arrived[row] = outgoing[row]
    v_out[...] = velocity
    for step in range(STEPS):
        for peer in row_peers:
            gather_copy(step, peer, row).wait_send()
        for peer in col_peers:
            scatter_copy(step, peer, col).wait_send()
    for peer in row_peers:
        exchange_copy(peer, peer).wait_recv()
    deck_out[...] = dot(gaps[...], arrived[...].reshape(n_row * LANE_ROWS, reals), EXACT)
    for peer in row_peers:
        exchange_copy(peer, row).wait_send()


def body(
    n_row, n_col,
    kernel, history, displacement, velocity, acceleration, excitation, solve_inverse, stiffness, owned, links, arms,
):
    lags = kernel.shape[0]
    slab, reals = velocity.shape
    modules = slab // 6
    block = kernel.shape[3]
    depth = n_row * slab
    points = modules * POINTS * 3
    anywhere = pl.BlockSpec(memory_space=pl.ANY)
    in_vmem = pl.BlockSpec(memory_space=pltpu.VMEM)
    groups = [(k, min(k + 3, lags)) for k in range(1, lags, 3)]
    bf16, fp32, i32 = jnp.bfloat16, jnp.float32, jnp.int32
    vm = pltpu.VMEM
    owned = owned.reshape(n_row, n_col * modules)
    v_last, gaps = pl.pallas_call(
        functools.partial(steps_kernel, n_row, n_col, lags, groups),
        out_shape=(
            jax.ShapeDtypeStruct((slab, reals), fp32),
            jax.ShapeDtypeStruct((points, reals), fp32),
        ),
        in_specs=[anywhere] * 11,
        out_specs=(in_vmem, in_vmem),
        scratch_shapes=[
            vm(kernel.shape, bf16),
            vm(history.shape, bf16),
            vm((reals, (lags - 1) * depth), bf16),
            vm((slab, reals), fp32),
            vm((slab, reals), fp32),
            vm((slab, reals), fp32),
            vm(excitation.shape, fp32),
            vm(solve_inverse.shape, fp32),
            vm(stiffness.shape, fp32),
            vm(owned.shape, i32),
            vm(links.shape, i32),
            vm(arms.shape, fp32),
            vm((3, block, depth), bf16),
            vm((reals, block), fp32),
            vm((STEPS, block, reals), fp32),
            vm((STEPS, n_col, slab, reals), fp32),
            vm((STEPS, slab, reals), bf16),
            vm((STEPS, n_row, slab, reals), bf16),
            vm((STEPS, n_col, slab, reals), fp32),
            vm((n_row, LANE_ROWS, reals), fp32),
            vm((n_row, LANE_ROWS, reals), fp32),
            vm((points, n_row * LANE_ROWS), fp32),
            vm((n_row * LANE_ROWS, slab), fp32),
            pltpu.SemaphoreType.DMA((32,)),
            pltpu.SemaphoreType.DMA((STEPS, n_row)),
            pltpu.SemaphoreType.DMA((STEPS, n_row)),
            pltpu.SemaphoreType.DMA((STEPS, n_col)),
            pltpu.SemaphoreType.DMA((STEPS, n_col)),
            pltpu.SemaphoreType.DMA((n_row,)),
            pltpu.SemaphoreType.DMA((n_row,)),
        ],
        compiler_params=pltpu.CompilerParams(
            collective_id=0, has_side_effects=True, vmem_limit_bytes=56 * 1024 * 1024
        ),
    )(kernel, history, displacement, velocity, acceleration, excitation, solve_inverse, stiffness, owned, links, arms)
    return v_last, gaps.reshape(modules, POINTS, 3, reals)


def solution(mesh):
    placed = (
        P(None, None, "col", "row"),
        P(None, None, "col", "sea"),
        P(("row", "col"), "sea"),
        P(("row", "col"), "sea"),
        P(("row", "col"), "sea"),
        P(None, ("row", "col"), "sea"),
        P(("row", "col"), None, None),
        P(("row", "col"), None, None),
        P(),
        P(("row", "col"), None),
        P(("row", "col"), None, None),
    )
    return jax.shard_map(
        functools.partial(body, mesh.shape["row"], mesh.shape["col"]),
        mesh=mesh,
        in_specs=placed,
        out_specs=(P(("row", "col"), "sea"), P(("row", "col"), None, None, "sea")),
        check_vma=False,
    )
```

```python
import functools

import jax
import jax.numpy as jnp
from jax import lax
from jax.experimental import pallas as pl
from jax.experimental.pallas import tpu as pltpu
from jax.sharding import PartitionSpec as P

POINTS = 16
STEPS = 3
SLOTS = 2
LANE_ROWS = 16

DT = 0.5
QUARTER = DT * DT / 4.0
TOP = 32000.0
PAIR = 2
MESH = pl.DeviceIdType.MESH
EXACT = lax.Precision.HIGHEST


def iota(shape, dim):
    return lax.broadcasted_iota(jnp.int32, shape, dim)


def f32(mask):
    return jnp.where(mask, 1.0, 0.0).astype(jnp.float32)


def dot(a, b, precision=None):
    return lax.dot_general(
        a, b, (((1,), (0,)), ((), ())), precision=precision, preferred_element_type=jnp.float32
    )


def dot_nt(a, b, precision=None):
    return lax.dot_general(
        a, b, (((1,), (1,)), ((), ())), precision=precision, preferred_element_type=jnp.float32
    )


def pieces(value, count):
    out = []
    for _ in range(count):
        out.append(value.astype(jnp.bfloat16))
        value = value - out[-1].astype(jnp.float32)
    return out


def left_pieces(matrix):
    high, low = pieces(matrix, 2)
    return jnp.concatenate([high, high, low, low], axis=1)


def right_pieces(matrix):
    high, low = pieces(matrix, 2)
    return jnp.concatenate([high, low, high, low], axis=0)


def block_diagonal(ref, modules):
    size = 6 * modules
    column = iota((size, size), 1)
    repeat = f32(iota((6, size), 1) % 6 == iota((6, size), 0))
    by_row = dot(ref[...].reshape(size, 6), repeat, EXACT)
    by_row = jnp.where(column // 6 == iota((size, size), 0) % modules, by_row, 0.0)
    order = f32(column == iota((size, size), 0) % 6 * modules + iota((size, size), 0) // 6)
    return dot(order, by_row, EXACT)


def routing_matrix(owned, base, modules):
    n_row, lanes = owned.shape
    lane = iota((n_row, lanes), 1)
    column = iota((n_row, modules), 1)
    out_rows = n_row * LANE_ROWS
    spread = f32(iota((modules, 6 * modules), 1) // 6 == iota((modules, 6 * modules), 0))
    total = jnp.zeros((out_rows, 6 * modules), jnp.float32)
    for slot in range(SLOTS):
        hit = jnp.zeros((n_row, modules), jnp.float32)
        for m in range(modules):
            here = f32((owned == base + m) & (lane % SLOTS == slot))
            hit = jnp.where(column == m, jnp.sum(here, axis=1, keepdims=True), hit)
        r = iota((out_rows, n_row), 0)
        lift = f32(
            (r // LANE_ROWS == iota((out_rows, n_row), 1))
            & (r % LANE_ROWS >= 6 * slot)
            & (r % LANE_ROWS < 6 * slot + 6)
        )
        wide = dot(dot(lift, hit), spread)
        rr = iota((out_rows, 6 * modules), 0) % LANE_ROWS - 6 * slot
        total = total + jnp.where(rr == iota((out_rows, 6 * modules), 1) % 6, wide, 0.0)
    return total


def choice_matrix(owned, row, col, home_size, modules):
    n_row, lanes = owned.shape
    home = owned // home_size
    mine = jnp.sum(jnp.where(iota((n_row, lanes), 0) == row, home, 0), axis=0, keepdims=True)
    per_lane = f32(iota((n_row, lanes), 0) == mine)
    size = 6 * modules
    pick = f32(iota((size, lanes), 1) == col * modules + iota((size, lanes), 0) // 6)
    by_row = dot_nt(pick, per_lane)
    out = n_row * LANE_ROWS
    widen = f32(iota((n_row, out), 1) // LANE_ROWS == iota((n_row, out), 0))
    wide = dot(by_row, widen)
    i = iota((size, out), 0)
    fits = iota((size, out), 1) % LANE_ROWS == 6 * (i // 6 % SLOTS) + i % 6
    return jnp.where(fits, wide, 0.0)


def gap_matrix(links_ref, arms_ref, first_point, modules):
    rows, size = 3 * POINTS, 6 * modules
    by_point = f32(iota((rows, POINTS), 0) % POINTS == iota((rows, POINTS), 1))
    levers = dot_nt(by_point, arms_ref[...].reshape(3 * modules, POINTS), EXACT)
    lane = iota((rows, size), 1)
    comp = iota((rows, size), 0) // POINTS
    mode = lane % 6
    spread = f32(iota((modules, size), 1) // 6 == iota((modules, size), 0))
    form = f32(mode == comp)
    for d in range(3):
        along = dot(levers[:, d * modules : (d + 1) * modules], spread, EXACT)
        form = form + jnp.where((mode == 3 + (comp + 1) % 3) & ((comp + 2) % 3 == d), along, 0.0)
        form = form - jnp.where((mode == 3 + (comp + 2) % 3) & ((comp + 1) % 3 == d), along, 0.0)
    local = (links_ref[...] - first_point).astype(jnp.float32)
    partner = dot_nt(by_point, local, EXACT).astype(jnp.int32)
    wide = iota((rows, rows), 1)
    same = wide // POINTS == iota((rows, rows), 0) // POINTS
    picks = [f32((partner[:, t : t + 1] % POINTS == wide % POINTS) & same) for t in range(modules)]
    other = dot(jnp.concatenate(picks, axis=0), form, EXACT)
    out = []
    for t in range(modules):
        theirs = other[t * rows : (t + 1) * rows]
        out.append(
            jnp.where(lane // 6 == t, form, 0.0)
            - jnp.where(lane // 6 == partner[:, t : t + 1] // POINTS, theirs, 0.0)
        )
    return jnp.concatenate(out, axis=0)


def coded(value, top):
    scale = jnp.where(top > 1e-30, TOP / jnp.maximum(top, 1e-30), 0.0)
    return jnp.round(value * scale).astype(jnp.int32).astype(jnp.int16)


def decoded(code, top):
    return code.astype(jnp.int32).astype(jnp.float32) * (top * (1.0 / TOP))


def largest(value):
    flat = value.reshape(-1, value.shape[-1])
    return jnp.max(jnp.abs(flat), axis=0, keepdims=True)


def steps_kernel(
    n_row, n_col, lags, groups,
    kernel_hbm, history_hbm, x_hbm, v_hbm, a_hbm, exc_hbm, solve_hbm, stiff_hbm, owned_hbm, links_hbm, arms_hbm,
    v_out, deck_out,
    kern, hist, past_t, x, v, a, exc, solve, stiff, owned, links, arms,
    k_t, acc, base_force, own_force, newest, window, pair_out, pair_in, line_out, line_in, outgoing, arrived,
    gaps, routing, pair_top_out, pair_top_in, line_top_out, line_top_in,
    local_sem, ag_send, ag_recv, pair_send, pair_recv, line_send, line_recv, top_send, top_recv, ex_send, ex_recv,
):
    row, col = lax.axis_index("row"), lax.axis_index("col")
    slab, reals = v.shape
    modules = slab // 6
    depth = n_row * slab
    block = n_col * slab
    half = block // PAIR
    n_line = n_col // PAIR
    grid_index = row * n_col + col
    line, side = col // PAIR, lax.rem(col, PAIR)
    other = 1 - side
    partner = line * PAIR + other

    sems = iter(range(64))

    def fetch(src, dst):
        copy = pltpu.make_async_copy(src, dst, local_sem.at[next(sems)])
        copy.start()
        return copy

    get_v = fetch(v_hbm, v)
    get_first = fetch(kernel_hbm.at[pl.ds(0, 1)], kern.at[pl.ds(0, 1)])
    get_groups = []
    for first, last in groups:
        get_groups.append(
            (
                fetch(history_hbm.at[pl.ds(first - 1, last - first)], hist.at[pl.ds(first - 1, last - first)]),
                fetch(kernel_hbm.at[pl.ds(first, last - first)], kern.at[pl.ds(first, last - first)]),
            )
        )
    get_state = [fetch(x_hbm, x), fetch(a_hbm, a), fetch(exc_hbm, exc), fetch(solve_hbm, solve), fetch(stiff_hbm, stiff)]
    get_tables = [fetch(owned_hbm, owned), fetch(links_hbm, links), fetch(arms_hbm, arms)]

    row_peers = [lax.rem(row + d, n_row) for d in range(1, n_row)]
    far_first = sorted(range(1, n_line), key=lambda d: -min(d, n_line - d))
    line_peers = [lax.rem(line + d, n_line) for d in far_first]

    barrier = pltpu.get_barrier_semaphore()
    for peer in row_peers:
        pl.semaphore_signal(barrier, inc=1, device_id={"row": peer}, device_id_type=MESH)
    pl.semaphore_signal(barrier, inc=1, device_id={"col": partner}, device_id_type=MESH)
    for peer in line_peers:
        pl.semaphore_signal(barrier, inc=1, device_id={"col": peer * PAIR + side}, device_id_type=MESH)
    pl.semaphore_wait(barrier, n_row - 1 + 1 + n_line - 1)

    def gather_copy(step, peer, source):
        return pltpu.make_async_remote_copy(
            src_ref=newest.at[step],
            dst_ref=window.at[step, source],
            send_sem=ag_send.at[step, peer],
            recv_sem=ag_recv.at[step, source],
            device_id={"row": peer},
            device_id_type=MESH,
        )

    def start_gather(step, value):
        newest[step] = value
        for peer in row_peers:
            gather_copy(step, peer, row).start()
        window[step, row] = value

    def wait_gather(step):
        for peer in row_peers:
            gather_copy(step, peer, peer).wait_recv()

    def pair_copy(step, piece):
        return pltpu.make_async_remote_copy(
            src_ref=pair_out.at[step, piece],
            dst_ref=pair_in.at[step, piece],
            send_sem=pair_send.at[step, piece],
            recv_sem=pair_recv.at[step, piece],
            device_id={"col": partner},
            device_id_type=MESH,
        )

    def pair_top_copy(step):
        return pltpu.make_async_remote_copy(
            src_ref=pair_top_out.at[step],
            dst_ref=pair_top_in.at[step],
            send_sem=top_send.at[step, n_line],
            recv_sem=top_recv.at[step, n_line],
            device_id={"col": partner},
            device_id_type=MESH,
        )

    def line_copy(step, peer, source):
        return pltpu.make_async_remote_copy(
            src_ref=line_out.at[step, peer],
            dst_ref=line_in.at[step, source],
            send_sem=line_send.at[step, peer],
            recv_sem=line_recv.at[step, source],
            device_id={"col": peer * PAIR + side},
            device_id_type=MESH,
        )

    def line_top_copy(step, peer, source):
        return pltpu.make_async_remote_copy(
            src_ref=line_top_out.at[step],
            dst_ref=line_top_in.at[step, source],
            send_sem=top_send.at[step, peer],
            recv_sem=top_recv.at[step, source],
            device_id={"col": peer * PAIR + side},
            device_id_type=MESH,
        )

    def exchange_copy(peer, source):
        return pltpu.make_async_remote_copy(
            src_ref=outgoing.at[peer],
            dst_ref=arrived.at[source],
            send_sem=ex_send.at[peer],
            recv_sem=ex_recv.at[source],
            device_id={"row": peer},
            device_id_type=MESH,
        )

    def window_of(step):
        return window[step].reshape(depth, reals)

    def lag_share(step, first, last):
        low = (first + 1 - step) * depth
        high = (last + 1 - step) * depth
        lag_block = kern[first:last].reshape((last - first) * depth, block)
        return dot(past_t[:, low:high], lag_block)

    def add_lags(step, index, fresh):
        share = lag_share(step, *groups[index])
        if fresh:
            acc[...] = share
        else:
            acc[...] += share

    def close_lags(step):
        base_force[step] = acc[...].T.reshape(n_line, PAIR, slab, reals)

    get_v.wait()
    start_gather(0, v[...].astype(jnp.bfloat16))
    get_first.wait()
    k_t[...] = kern[0].reshape(depth, block).T.reshape(n_line, PAIR, slab, depth)
    for index, (first, last) in enumerate(groups):
        for copy in get_groups[index]:
            copy.wait()
        for k in range(first - 1, last - 1):
            past_t[:, (k + 2) * depth : (k + 3) * depth] = hist[k].reshape(depth, reals).T
        add_lags(0, index, index == 0)
    close_lags(0)

    def half_force(step, which):
        now = dot(k_t[:, which].reshape(half, depth), window_of(step))
        return base_force[step, :, which] + now.reshape(n_line, slab, reals)

    def send_force(step):
        wait_gather(step)
        theirs = half_force(step, other)
        top = largest(theirs)
        pair_top_out[step] = top
        pair_top_copy(step).start()
        own_force[...] = theirs
        for piece in [*line_peers, line]:
            pair_out[step, piece] = coded(own_force[piece], top)
            pair_copy(step, piece).start()
        mine = half_force(step, side)
        own_force[...] = mine
        return largest(mine)

    def pass_on(step, own_top, fillers):
        fillers = list(fillers)
        pair_top_copy(step).wait_recv()
        top_in = pair_top_in[step]
        top = own_top + top_in
        line_top_out[step] = top
        for peer in line_peers:
            line_top_copy(step, peer, line).start()
        for peer in line_peers:
            pair_copy(step, peer).wait_recv()
            line_out[step, peer] = coded(own_force[peer] + decoded(pair_in[step, peer], top_in), top)
            line_copy(step, peer, line).start()
            if fillers:
                fillers.pop(0)()
        pair_copy(step, line).wait_recv()
        total = own_force[line] + decoded(pair_in[step, line], top_in)
        own_force[line] = total
        for filler in fillers:
            filler()
        total = own_force[line]
        for peer in line_peers:
            line_top_copy(step, peer, peer).wait_recv()
            line_copy(step, peer, peer).wait_recv()
            total = total + decoded(line_in[step, peer], line_top_in[step, peer])
        return total

    own_top = send_force(0)

    for copy in get_state:
        copy.wait()
    solve_left = left_pieces(block_diagonal(solve, modules))
    stiff_left = left_pieces(block_diagonal(stiff, modules))

    def newest_past(step):
        past_t[:, (1 - step) * depth : (2 - step) * depth] = window_of(step).T

    def fill_lags(step):
        order = [*range(1, len(groups)), 0]
        return [functools.partial(add_lags, step, index, i == 0) for i, index in enumerate(order)] + [
            functools.partial(close_lags, step)
        ]

    def tables():
        for copy in get_tables:
            copy.wait()
        route = routing_matrix(owned[...], grid_index * modules, modules).astype(jnp.bfloat16)
        routing[...] = jnp.concatenate([route, route, route], axis=1)
        forms = dot(
            gap_matrix(links, arms, grid_index * modules * POINTS, modules),
            choice_matrix(owned[...], row, col, n_col * modules, modules),
            EXACT,
        )
        gaps[...] = left_pieces(forms)

    displacement, velocity, acceleration = x[...], v[...], a[...]
    for step in range(STEPS):
        predicted = displacement + DT * velocity + QUARTER * acceleration
        known = dot(solve_left, right_pieces(exc[step] - dot(stiff_left, right_pieces(predicted))))
        drift = velocity + 0.5 * DT * (acceleration + known)
        if step + 1 < STEPS:
            newest_past(step)
        total = pass_on(step, own_top, fill_lags(step + 1) if step + 1 < STEPS else [tables])
        answer = dot(solve_left, right_pieces(total))
        velocity = drift - 0.5 * DT * answer
        if step + 1 < STEPS:
            start_gather(step + 1, velocity.astype(jnp.bfloat16))
        acceleration = known - answer
        displacement = predicted + QUARTER * acceleration
        if step + 1 < STEPS:
            own_top = send_force(step + 1)

    leaving = dot(routing[...], jnp.concatenate(pieces(displacement, 3), axis=0))
    outgoing[...] = leaving.reshape(n_row, LANE_ROWS, reals)
    for peer in row_peers:
        exchange_copy(peer, row).start()
    arrived[row] = outgoing[row]
    v_out[...] = velocity
    for step in range(STEPS):
        for peer in row_peers:
            gather_copy(step, peer, row).wait_send()
        pair_top_copy(step).wait_send()
        for piece in [*line_peers, line]:
            pair_copy(step, piece).wait_send()
        for peer in line_peers:
            line_top_copy(step, peer, line).wait_send()
            line_copy(step, peer, line).wait_send()
    for peer in row_peers:
        exchange_copy(peer, peer).wait_recv()
    deck_out[...] = dot(gaps[...], right_pieces(arrived[...].reshape(n_row * LANE_ROWS, reals)))
    for peer in row_peers:
        exchange_copy(peer, row).wait_send()


def body(
    n_row, n_col,
    kernel, history, displacement, velocity, acceleration, excitation, solve_inverse, stiffness, owned, links, arms,
):
    lags = kernel.shape[0]
    slab, reals = velocity.shape
    modules = slab // 6
    block = kernel.shape[3]
    depth = n_row * slab
    n_line = n_col // PAIR
    points = modules * POINTS * 3
    arrivals = n_row * LANE_ROWS
    anywhere = pl.BlockSpec(memory_space=pl.ANY)
    in_vmem = pl.BlockSpec(memory_space=pltpu.VMEM)
    groups = [(1, 2)] + [(k, min(k + 2, lags)) for k in range(2, lags, 2)]
    bf16, fp32, i32, i16 = jnp.bfloat16, jnp.float32, jnp.int32, jnp.int16
    vm = pltpu.VMEM
    sems = pltpu.SemaphoreType.DMA
    owned = owned.reshape(n_row, n_col * modules)
    solve_inverse = solve_inverse.transpose(1, 0, 2)
    stiffness = stiffness.transpose(1, 0, 2)
    arms = arms.transpose(1, 0, 2)
    v_last, gaps = pl.pallas_call(
        functools.partial(steps_kernel, n_row, n_col, lags, groups),
        out_shape=(
            jax.ShapeDtypeStruct((slab, reals), fp32),
            jax.ShapeDtypeStruct((points, reals), fp32),
        ),
        in_specs=[anywhere] * 11,
        out_specs=(in_vmem, in_vmem),
        scratch_shapes=[
            vm(kernel.shape, bf16),
            vm(history.shape, bf16),
            vm((reals, (lags + 1) * depth), bf16),
            vm((slab, reals), fp32),
            vm((slab, reals), fp32),
            vm((slab, reals), fp32),
            vm(excitation.shape, fp32),
            vm(solve_inverse.shape, fp32),
            vm(stiffness.shape, fp32),
            vm(owned.shape, i32),
            vm(links.shape, i32),
            vm(arms.shape, fp32),
            vm((n_line, PAIR, slab, depth), bf16),
            vm((reals, block), fp32),
            vm((STEPS, n_line, PAIR, slab, reals), fp32),
            vm((n_line, slab, reals), fp32),
            vm((STEPS, slab, reals), bf16),
            vm((STEPS, n_row, slab, reals), bf16),
            vm((STEPS, n_line, slab, reals), i16),
            vm((STEPS, n_line, slab, reals), i16),
            vm((STEPS, n_line, slab, reals), i16),
            vm((STEPS, n_line, slab, reals), i16),
            vm((n_row, LANE_ROWS, reals), fp32),
            vm((n_row, LANE_ROWS, reals), fp32),
            vm((points, 4 * arrivals), bf16),
            vm((arrivals, 3 * slab), bf16),
            vm((STEPS, 1, reals), fp32),
            vm((STEPS, 1, reals), fp32),
            vm((STEPS, 1, reals), fp32),
            vm((STEPS, n_line, 1, reals), fp32),
            sems((32,)),
            sems((STEPS, n_row)),
            sems((STEPS, n_row)),
            sems((STEPS, n_line)),
            sems((STEPS, n_line)),
            sems((STEPS, n_line)),
            sems((STEPS, n_line)),
            sems((STEPS, n_line + 1)),
            sems((STEPS, n_line + 1)),
            sems((n_row,)),
            sems((n_row,)),
        ],
        compiler_params=pltpu.CompilerParams(
            collective_id=0, has_side_effects=True, vmem_limit_bytes=56 * 1024 * 1024
        ),
    )(kernel, history, displacement, velocity, acceleration, excitation, solve_inverse, stiffness, owned, links, arms)
    return v_last, gaps.reshape(modules, 3, POINTS, reals).transpose(0, 2, 1, 3)


def solution(mesh):
    placed = (
        P(None, None, "col", "row"),
        P(None, None, "col", "sea"),
        P(("row", "col"), "sea"),
        P(("row", "col"), "sea"),
        P(("row", "col"), "sea"),
        P(None, ("row", "col"), "sea"),
        P(("row", "col"), None, None),
        P(("row", "col"), None, None),
        P(),
        P(("row", "col"), None),
        P(("row", "col"), None, None),
    )
    return jax.shard_map(
        functools.partial(body, mesh.shape["row"], mesh.shape["col"]),
        mesh=mesh,
        in_specs=placed,
        out_specs=(P(("row", "col"), "sea"), P(("row", "col"), None, None, "sea")),
        check_vma=False,
    )
```

```python
import functools

import jax
import jax.numpy as jnp
from jax import lax
from jax.experimental import pallas as pl
from jax.experimental.pallas import tpu as pltpu
from jax.sharding import PartitionSpec as P

POINTS = 16
STEPS = 3
SLOTS = 2
LANE_ROWS = 16

DT = 0.5
QUARTER = DT * DT / 4.0
TOP = 32000.0
PAIR = 2
ROW_RING = 4
MESH = pl.DeviceIdType.MESH
EXACT = lax.Precision.HIGHEST


def iota(shape, dim):
    return lax.broadcasted_iota(jnp.int32, shape, dim)


def f32(mask):
    return jnp.where(mask, 1.0, 0.0).astype(jnp.float32)


def dot(a, b, precision=None):
    return lax.dot_general(
        a, b, (((1,), (0,)), ((), ())), precision=precision, preferred_element_type=jnp.float32
    )


def dot_nt(a, b, precision=None):
    return lax.dot_general(
        a, b, (((1,), (1,)), ((), ())), precision=precision, preferred_element_type=jnp.float32
    )


def pieces(value, count):
    out = []
    for _ in range(count):
        out.append(value.astype(jnp.bfloat16))
        value = value - out[-1].astype(jnp.float32)
    return out


def left_pieces(matrix):
    high, low = pieces(matrix, 2)
    return jnp.concatenate([high, high, low, low], axis=1)


def right_pieces(matrix):
    high, low = pieces(matrix, 2)
    return jnp.concatenate([high, low, high, low], axis=0)


def block_diagonal(ref, modules):
    size = 6 * modules
    column = iota((size, size), 1)
    repeat = f32(iota((6, size), 1) % 6 == iota((6, size), 0))
    by_row = dot(ref[...].reshape(size, 6), repeat, EXACT)
    by_row = jnp.where(column // 6 == iota((size, size), 0) % modules, by_row, 0.0)
    order = f32(column == iota((size, size), 0) % 6 * modules + iota((size, size), 0) // 6)
    return dot(order, by_row, EXACT)


def routing_matrix(owned, base, modules):
    n_row, lanes = owned.shape
    lane = iota((n_row, lanes), 1)
    column = iota((n_row, modules), 1)
    out_rows = n_row * LANE_ROWS
    spread = f32(iota((modules, 6 * modules), 1) // 6 == iota((modules, 6 * modules), 0))
    total = jnp.zeros((out_rows, 6 * modules), jnp.float32)
    for slot in range(SLOTS):
        hit = jnp.zeros((n_row, modules), jnp.float32)
        for m in range(modules):
            here = f32((owned == base + m) & (lane % SLOTS == slot))
            hit = jnp.where(column == m, jnp.sum(here, axis=1, keepdims=True), hit)
        r = iota((out_rows, n_row), 0)
        lift = f32(
            (r // LANE_ROWS == iota((out_rows, n_row), 1))
            & (r % LANE_ROWS >= 6 * slot)
            & (r % LANE_ROWS < 6 * slot + 6)
        )
        wide = dot(dot(lift, hit), spread)
        rr = iota((out_rows, 6 * modules), 0) % LANE_ROWS - 6 * slot
        total = total + jnp.where(rr == iota((out_rows, 6 * modules), 1) % 6, wide, 0.0)
    return total


def choice_matrix(owned, row, col, home_size, modules):
    n_row, lanes = owned.shape
    home = owned // home_size
    mine = jnp.sum(jnp.where(iota((n_row, lanes), 0) == row, home, 0), axis=0, keepdims=True)
    per_lane = f32(iota((n_row, lanes), 0) == mine)
    size = 6 * modules
    pick = f32(iota((size, lanes), 1) == col * modules + iota((size, lanes), 0) // 6)
    by_row = dot_nt(pick, per_lane)
    out = n_row * LANE_ROWS
    widen = f32(iota((n_row, out), 1) // LANE_ROWS == iota((n_row, out), 0))
    wide = dot(by_row, widen)
    i = iota((size, out), 0)
    fits = iota((size, out), 1) % LANE_ROWS == 6 * (i // 6 % SLOTS) + i % 6
    return jnp.where(fits, wide, 0.0)


def gap_matrix(links_ref, arms_ref, first_point, modules):
    rows, size = 3 * POINTS, 6 * modules
    by_point = f32(iota((rows, POINTS), 0) % POINTS == iota((rows, POINTS), 1))
    levers = dot_nt(by_point, arms_ref[...].reshape(3 * modules, POINTS), EXACT)
    lane = iota((rows, size), 1)
    comp = iota((rows, size), 0) // POINTS
    mode = lane % 6
    spread = f32(iota((modules, size), 1) // 6 == iota((modules, size), 0))
    form = f32(mode == comp)
    for d in range(3):
        along = dot(levers[:, d * modules : (d + 1) * modules], spread, EXACT)
        form = form + jnp.where((mode == 3 + (comp + 1) % 3) & ((comp + 2) % 3 == d), along, 0.0)
        form = form - jnp.where((mode == 3 + (comp + 2) % 3) & ((comp + 1) % 3 == d), along, 0.0)
    local = (links_ref[...] - first_point).astype(jnp.float32)
    partner = dot_nt(by_point, local, EXACT).astype(jnp.int32)
    wide = iota((rows, rows), 1)
    same = wide // POINTS == iota((rows, rows), 0) // POINTS
    picks = [f32((partner[:, t : t + 1] % POINTS == wide % POINTS) & same) for t in range(modules)]
    other = dot(jnp.concatenate(picks, axis=0), form, EXACT)
    out = []
    for t in range(modules):
        theirs = other[t * rows : (t + 1) * rows]
        out.append(
            jnp.where(lane // 6 == t, form, 0.0)
            - jnp.where(lane // 6 == partner[:, t : t + 1] // POINTS, theirs, 0.0)
        )
    return jnp.concatenate(out, axis=0)


def coded(value, top):
    scale = jnp.where(top > 1e-30, TOP / jnp.maximum(top, 1e-30), 0.0)
    return jnp.round(value * scale).astype(jnp.int32).astype(jnp.int16)


def decoded(code, top):
    return code.astype(jnp.int32).astype(jnp.float32) * (top * (1.0 / TOP))


def largest(value):
    flat = value.reshape(-1, value.shape[-1])
    return jnp.max(jnp.abs(flat), axis=0, keepdims=True)


def steps_kernel(
    n_row, n_col, lags, groups,
    kernel_hbm, history_hbm, x_hbm, v_hbm, a_hbm, exc_hbm, solve_hbm, stiff_hbm, owned_hbm, links_hbm, arms_hbm,
    v_out, deck_out,
    kern, hist, past_t, x, v, a, exc, solve, stiff, owned, links, arms,
    k_t, acc, base_force, own_force, newest, window, pair_out, pair_in, line_out, line_in, outgoing, arrived,
    gaps, routing, pair_top_out, pair_top_in, line_top_out, line_top_in,
    local_sem, ag_send, ag_recv, pair_send, pair_recv, line_send, line_recv, top_send, top_recv, ex_send, ex_recv,
):
    row, col = lax.axis_index("row"), lax.axis_index("col")
    slab, reals = v.shape
    modules = slab // 6
    depth = n_row * slab
    block = n_col * slab
    half = block // PAIR
    n_line = n_col // PAIR
    grid_index = row * n_col + col
    line, side = col // PAIR, lax.rem(col, PAIR)
    other = 1 - side
    partner = line * PAIR + other

    sems = iter(range(64))

    def fetch(src, dst):
        copy = pltpu.make_async_copy(src, dst, local_sem.at[next(sems)])
        copy.start()
        return copy

    get_v = fetch(v_hbm, v)
    get_first = fetch(kernel_hbm.at[pl.ds(0, 1)], kern.at[pl.ds(0, 1)])
    get_groups = []
    for first, last in groups:
        get_groups.append(
            (
                fetch(history_hbm.at[pl.ds(first - 1, last - first)], hist.at[pl.ds(first - 1, last - first)]),
                fetch(kernel_hbm.at[pl.ds(first, last - first)], kern.at[pl.ds(first, last - first)]),
            )
        )
    get_state = [fetch(x_hbm, x), fetch(a_hbm, a), fetch(exc_hbm, exc), fetch(solve_hbm, solve), fetch(stiff_hbm, stiff)]
    get_tables = [fetch(owned_hbm, owned), fetch(links_hbm, links), fetch(arms_hbm, arms)]

    ring, turn = row % ROW_RING, row // ROW_RING
    row_peers = [
        lax.rem(turn + t, n_row // ROW_RING) * ROW_RING + lax.rem(ring + d, ROW_RING)
        for t in (1, 0)
        for d in (2, 1, 3, 0)
        if t or d
    ]
    far_first = sorted(range(1, n_line), key=lambda d: -min(d, n_line - d))
    line_peers = [lax.rem(line + d, n_line) for d in far_first]

    barrier = pltpu.get_barrier_semaphore()
    for peer in row_peers:
        pl.semaphore_signal(barrier, inc=1, device_id={"row": peer}, device_id_type=MESH)
    pl.semaphore_signal(barrier, inc=1, device_id={"col": partner}, device_id_type=MESH)
    for peer in line_peers:
        pl.semaphore_signal(barrier, inc=1, device_id={"col": peer * PAIR + side}, device_id_type=MESH)
    pl.semaphore_wait(barrier, n_row - 1 + 1 + n_line - 1)

    def gather_copy(step, peer, source):
        return pltpu.make_async_remote_copy(
            src_ref=newest.at[step],
            dst_ref=window.at[step, source],
            send_sem=ag_send.at[step, peer],
            recv_sem=ag_recv.at[step, source],
            device_id={"row": peer},
            device_id_type=MESH,
        )

    def start_gather(step, value):
        newest[step] = value
        for peer in row_peers:
            gather_copy(step, peer, row).start()
        window[step, row] = value

    def wait_gather(step):
        for peer in row_peers:
            gather_copy(step, peer, peer).wait_recv()

    def pair_copy(step, piece):
        return pltpu.make_async_remote_copy(
            src_ref=pair_out.at[step, piece],
            dst_ref=pair_in.at[step, piece],
            send_sem=pair_send.at[step, piece],
            recv_sem=pair_recv.at[step, piece],
            device_id={"col": partner},
            device_id_type=MESH,
        )

    def pair_top_copy(step):
        return pltpu.make_async_remote_copy(
            src_ref=pair_top_out.at[step],
            dst_ref=pair_top_in.at[step],
            send_sem=top_send.at[step, n_line],
            recv_sem=top_recv.at[step, n_line],
            device_id={"col": partner},
            device_id_type=MESH,
        )

    def line_copy(step, peer, source):
        return pltpu.make_async_remote_copy(
            src_ref=line_out.at[step, peer],
            dst_ref=line_in.at[step, source],
            send_sem=line_send.at[step, peer],
            recv_sem=line_recv.at[step, source],
            device_id={"col": peer * PAIR + side},
            device_id_type=MESH,
        )

    def line_top_copy(step, peer, source):
        return pltpu.make_async_remote_copy(
            src_ref=line_top_out.at[step],
            dst_ref=line_top_in.at[step, source],
            send_sem=top_send.at[step, peer],
            recv_sem=top_recv.at[step, source],
            device_id={"col": peer * PAIR + side},
            device_id_type=MESH,
        )

    def exchange_copy(peer, source):
        return pltpu.make_async_remote_copy(
            src_ref=outgoing.at[peer],
            dst_ref=arrived.at[source],
            send_sem=ex_send.at[peer],
            recv_sem=ex_recv.at[source],
            device_id={"row": peer},
            device_id_type=MESH,
        )

    def window_of(step):
        return window[step].reshape(depth, reals)

    def lag_share(step, first, last):
        low = (first + 1 - step) * depth
        high = (last + 1 - step) * depth
        lag_block = kern[first:last].reshape((last - first) * depth, block)
        return dot(past_t[:, low:high], lag_block)

    def add_lags(step, index, fresh):
        share = lag_share(step, *groups[index])
        if fresh:
            acc[...] = share
        else:
            acc[...] += share

    def close_lags(step):
        base_force[step] = acc[...].T.reshape(n_line, PAIR, slab, reals)

    get_v.wait()
    start_gather(0, v[...].astype(jnp.bfloat16))
    get_first.wait()
    k_t[...] = kern[0].reshape(depth, block).T.reshape(n_line, PAIR, slab, depth)
    for index, (first, last) in enumerate(groups):
        for copy in get_groups[index]:
            copy.wait()
        for k in range(first - 1, last - 1):
            past_t[:, (k + 2) * depth : (k + 3) * depth] = hist[k].reshape(depth, reals).T
        add_lags(0, index, index == 0)
    close_lags(0)

    def half_force(step, which):
        now = dot(k_t[:, which].reshape(half, depth), window_of(step))
        return base_force[step, :, which] + now.reshape(n_line, slab, reals)

    def send_force(step):
        wait_gather(step)
        theirs = half_force(step, other)
        top = largest(theirs)
        pair_top_out[step] = top
        pair_top_copy(step).start()
        own_force[...] = theirs
        for piece in [*line_peers, line]:
            pair_out[step, piece] = coded(own_force[piece], top)
            pair_copy(step, piece).start()
        mine = half_force(step, side)
        own_force[...] = mine
        return largest(mine)

    def pass_on(step, own_top, early, late):
        for filler in early:
            filler()
        pair_top_copy(step).wait_recv()
        top_in = pair_top_in[step]
        top = own_top + top_in
        line_top_out[step] = top
        for peer in line_peers:
            line_top_copy(step, peer, line).start()
        for peer in line_peers:
            pair_copy(step, peer).wait_recv()
            line_out[step, peer] = coded(own_force[peer] + decoded(pair_in[step, peer], top_in), top)
            line_copy(step, peer, line).start()
        pair_copy(step, line).wait_recv()
        total = own_force[line] + decoded(pair_in[step, line], top_in)
        own_force[line] = total
        for filler in late:
            filler()
        total = own_force[line]
        for peer in line_peers:
            line_top_copy(step, peer, peer).wait_recv()
            line_copy(step, peer, peer).wait_recv()
            total = total + decoded(line_in[step, peer], line_top_in[step, peer])
        return total

    own_top = send_force(0)

    for copy in get_state:
        copy.wait()
    solve_left = left_pieces(block_diagonal(solve, modules))
    stiff_left = left_pieces(block_diagonal(stiff, modules))

    def newest_past(step):
        past_t[:, (1 - step) * depth : (2 - step) * depth] = window_of(step).T

    def tables():
        for copy in get_tables:
            copy.wait()
        route = routing_matrix(owned[...], grid_index * modules, modules).astype(jnp.bfloat16)
        routing[...] = jnp.concatenate([route, route, route], axis=1)
        forms = dot(
            gap_matrix(links, arms, grid_index * modules * POINTS, modules),
            choice_matrix(owned[...], row, col, n_col * modules, modules),
            EXACT,
        )
        gaps[...] = left_pieces(forms)

    def fill_lags(step):
        order = [*range(1, len(groups)), 0]
        return [functools.partial(add_lags, step, index, i == 0) for i, index in enumerate(order)] + [
            functools.partial(close_lags, step)
        ]

    fillers = [fill_lags(1), fill_lags(2), [tables]]
    early_ends, late_ends = (0, 1, 0), (3, 4, 1)


    displacement, velocity, acceleration = x[...], v[...], a[...]
    for step in range(STEPS):
        predicted = displacement + DT * velocity + QUARTER * acceleration
        known = dot(solve_left, right_pieces(exc[step] - dot(stiff_left, right_pieces(predicted))))
        drift = velocity + 0.5 * DT * (acceleration + known)
        if step + 1 < STEPS:
            newest_past(step)
        work = fillers[step]
        total = pass_on(step, own_top, work[: early_ends[step]], work[early_ends[step] : late_ends[step]])
        answer = dot(solve_left, right_pieces(total))
        velocity = drift - 0.5 * DT * answer
        if step + 1 < STEPS:
            start_gather(step + 1, velocity.astype(jnp.bfloat16))
        acceleration = known - answer
        displacement = predicted + QUARTER * acceleration
        for filler in work[late_ends[step] :]:
            filler()
        if step + 1 < STEPS:
            own_top = send_force(step + 1)

    leaving = dot(routing[...], jnp.concatenate(pieces(displacement, 3), axis=0))
    outgoing[...] = leaving.reshape(n_row, LANE_ROWS, reals)
    for peer in row_peers:
        exchange_copy(peer, row).start()
    arrived[row] = outgoing[row]
    v_out[...] = velocity
    for step in range(STEPS):
        for peer in row_peers:
            gather_copy(step, peer, row).wait_send()
        pair_top_copy(step).wait_send()
        for piece in [*line_peers, line]:
            pair_copy(step, piece).wait_send()
        for peer in line_peers:
            line_top_copy(step, peer, line).wait_send()
            line_copy(step, peer, line).wait_send()
    for peer in row_peers:
        exchange_copy(peer, peer).wait_recv()
    deck_out[...] = dot(gaps[...], right_pieces(arrived[...].reshape(n_row * LANE_ROWS, reals)))
    for peer in row_peers:
        exchange_copy(peer, row).wait_send()


def body(
    n_row, n_col,
    kernel, history, displacement, velocity, acceleration, excitation, solve_inverse, stiffness, owned, links, arms,
):
    lags = kernel.shape[0]
    slab, reals = velocity.shape
    modules = slab // 6
    block = kernel.shape[3]
    depth = n_row * slab
    n_line = n_col // PAIR
    points = modules * POINTS * 3
    arrivals = n_row * LANE_ROWS
    anywhere = pl.BlockSpec(memory_space=pl.ANY)
    in_vmem = pl.BlockSpec(memory_space=pltpu.VMEM)
    groups = [(1, 2)] + [(k, min(k + 4, lags)) for k in range(2, lags, 4)]
    bf16, fp32, i32, i16 = jnp.bfloat16, jnp.float32, jnp.int32, jnp.int16
    vm = pltpu.VMEM
    sems = pltpu.SemaphoreType.DMA
    owned = owned.reshape(n_row, n_col * modules)
    solve_inverse = solve_inverse.transpose(1, 0, 2)
    stiffness = stiffness.transpose(1, 0, 2)
    arms = arms.transpose(1, 0, 2)
    v_last, gaps = pl.pallas_call(
        functools.partial(steps_kernel, n_row, n_col, lags, groups),
        out_shape=(vm((slab, reals), fp32), vm((points, reals), fp32)),
        in_specs=[anywhere] * 11,
        out_specs=(in_vmem, in_vmem),
        scratch_shapes=[
            vm(kernel.shape, bf16),
            vm(history.shape, bf16),
            vm((reals, (lags + 1) * depth), bf16),
            vm((slab, reals), fp32),
            vm((slab, reals), fp32),
            vm((slab, reals), fp32),
            vm(excitation.shape, fp32),
            vm(solve_inverse.shape, fp32),
            vm(stiffness.shape, fp32),
            vm(owned.shape, i32),
            vm(links.shape, i32),
            vm(arms.shape, fp32),
            vm((n_line, PAIR, slab, depth), bf16),
            vm((reals, block), fp32),
            vm((STEPS, n_line, PAIR, slab, reals), fp32),
            vm((n_line, slab, reals), fp32),
            vm((STEPS, slab, reals), bf16),
            vm((STEPS, n_row, slab, reals), bf16),
            vm((STEPS, n_line, slab, reals), i16),
            vm((STEPS, n_line, slab, reals), i16),
            vm((STEPS, n_line, slab, reals), i16),
            vm((STEPS, n_line, slab, reals), i16),
            vm((n_row, LANE_ROWS, reals), fp32),
            vm((n_row, LANE_ROWS, reals), fp32),
            vm((points, 4 * arrivals), bf16),
            vm((arrivals, 3 * slab), bf16),
            vm((STEPS, 1, reals), fp32),
            vm((STEPS, 1, reals), fp32),
            vm((STEPS, 1, reals), fp32),
            vm((STEPS, n_line, 1, reals), fp32),
            sems((32,)),
            sems((STEPS, n_row)),
            sems((STEPS, n_row)),
            sems((STEPS, n_line)),
            sems((STEPS, n_line)),
            sems((STEPS, n_line)),
            sems((STEPS, n_line)),
            sems((STEPS, n_line + 1)),
            sems((STEPS, n_line + 1)),
            sems((n_row,)),
            sems((n_row,)),
        ],
        compiler_params=pltpu.CompilerParams(
            collective_id=0, has_side_effects=True, vmem_limit_bytes=56 * 1024 * 1024
        ),
    )(kernel, history, displacement, velocity, acceleration, excitation, solve_inverse, stiffness, owned, links, arms)
    return v_last, gaps.reshape(modules, 3, POINTS, reals).transpose(0, 2, 1, 3)


def solution(mesh):
    placed = (
        P(None, None, "col", "row"),
        P(None, None, "col", "sea"),
        P(("row", "col"), "sea"),
        P(("row", "col"), "sea"),
        P(("row", "col"), "sea"),
        P(None, ("row", "col"), "sea"),
        P(("row", "col"), None, None),
        P(("row", "col"), None, None),
        P(),
        P(("row", "col"), None),
        P(("row", "col"), None, None),
    )
    return jax.shard_map(
        functools.partial(body, mesh.shape["row"], mesh.shape["col"]),
        mesh=mesh,
        in_specs=placed,
        out_specs=(P(("row", "col"), "sea"), P(("row", "col"), None, None, "sea")),
        check_vma=False,
    )
```

```python
import functools

import jax
import jax.numpy as jnp
from jax import lax
from jax.experimental import pallas as pl
from jax.experimental.pallas import tpu as pltpu
from jax.sharding import PartitionSpec as P

POINTS = 16
STEPS = 3
SLOTS = 2
LANE_ROWS = 16

DT = 0.5
QUARTER = DT * DT / 4.0
TOP = 32000.0
PAIR = 2
ROW_RING = 4
PARTS = 2
MESH = pl.DeviceIdType.MESH
EXACT = lax.Precision.HIGHEST


def iota(shape, dim):
    return lax.broadcasted_iota(jnp.int32, shape, dim)


def f32(mask):
    return jnp.where(mask, 1.0, 0.0).astype(jnp.float32)


def dot(a, b, precision=None):
    return lax.dot_general(
        a, b, (((1,), (0,)), ((), ())), precision=precision, preferred_element_type=jnp.float32
    )


def dot_nt(a, b, precision=None):
    return lax.dot_general(
        a, b, (((1,), (1,)), ((), ())), precision=precision, preferred_element_type=jnp.float32
    )


def pieces(value, count):
    out = []
    for _ in range(count):
        out.append(value.astype(jnp.bfloat16))
        value = value - out[-1].astype(jnp.float32)
    return out


def left_pieces(matrix):
    high, low = pieces(matrix, 2)
    return jnp.concatenate([high, high, low, low], axis=1)


def right_pieces(matrix):
    high, low = pieces(matrix, 2)
    return jnp.concatenate([high, low, high, low], axis=0)


def block_diagonal(ref, modules):
    size = 6 * modules
    column = iota((size, size), 1)
    repeat = f32(iota((6, size), 1) % 6 == iota((6, size), 0))
    by_row = dot(ref[...].reshape(size, 6), repeat, EXACT)
    by_row = jnp.where(column // 6 == iota((size, size), 0) % modules, by_row, 0.0)
    order = f32(column == iota((size, size), 0) % 6 * modules + iota((size, size), 0) // 6)
    return dot(order, by_row, EXACT)


def routing_matrix(owned, base, modules):
    n_row, lanes = owned.shape
    lane = iota((n_row, lanes), 1)
    column = iota((n_row, modules), 1)
    out_rows = n_row * LANE_ROWS
    spread = f32(iota((modules, 6 * modules), 1) // 6 == iota((modules, 6 * modules), 0))
    total = jnp.zeros((out_rows, 6 * modules), jnp.float32)
    for slot in range(SLOTS):
        hit = jnp.zeros((n_row, modules), jnp.float32)
        for m in range(modules):
            here = f32((owned == base + m) & (lane % SLOTS == slot))
            hit = jnp.where(column == m, jnp.sum(here, axis=1, keepdims=True), hit)
        r = iota((out_rows, n_row), 0)
        lift = f32(
            (r // LANE_ROWS == iota((out_rows, n_row), 1))
            & (r % LANE_ROWS >= 6 * slot)
            & (r % LANE_ROWS < 6 * slot + 6)
        )
        wide = dot(dot(lift, hit), spread)
        rr = iota((out_rows, 6 * modules), 0) % LANE_ROWS - 6 * slot
        total = total + jnp.where(rr == iota((out_rows, 6 * modules), 1) % 6, wide, 0.0)
    return total


def choice_matrix(owned, row, col, home_size, modules):
    n_row, lanes = owned.shape
    home = owned // home_size
    mine = jnp.sum(jnp.where(iota((n_row, lanes), 0) == row, home, 0), axis=0, keepdims=True)
    per_lane = f32(iota((n_row, lanes), 0) == mine)
    size = 6 * modules
    pick = f32(iota((size, lanes), 1) == col * modules + iota((size, lanes), 0) // 6)
    by_row = dot_nt(pick, per_lane)
    out = n_row * LANE_ROWS
    widen = f32(iota((n_row, out), 1) // LANE_ROWS == iota((n_row, out), 0))
    wide = dot(by_row, widen)
    i = iota((size, out), 0)
    fits = iota((size, out), 1) % LANE_ROWS == 6 * (i // 6 % SLOTS) + i % 6
    return jnp.where(fits, wide, 0.0)


def gap_matrix(links_ref, arms_ref, first_point, modules):
    rows, size = 3 * POINTS, 6 * modules
    by_point = f32(iota((rows, POINTS), 0) % POINTS == iota((rows, POINTS), 1))
    levers = dot_nt(by_point, arms_ref[...].reshape(3 * modules, POINTS), EXACT)
    lane = iota((rows, size), 1)
    comp = iota((rows, size), 0) // POINTS
    mode = lane % 6
    spread = f32(iota((modules, size), 1) // 6 == iota((modules, size), 0))
    form = f32(mode == comp)
    for d in range(3):
        along = dot(levers[:, d * modules : (d + 1) * modules], spread, EXACT)
        form = form + jnp.where((mode == 3 + (comp + 1) % 3) & ((comp + 2) % 3 == d), along, 0.0)
        form = form - jnp.where((mode == 3 + (comp + 2) % 3) & ((comp + 1) % 3 == d), along, 0.0)
    local = (links_ref[...] - first_point).astype(jnp.float32)
    partner = dot_nt(by_point, local, EXACT).astype(jnp.int32)
    wide = iota((rows, rows), 1)
    same = wide // POINTS == iota((rows, rows), 0) // POINTS
    picks = [f32((partner[:, t : t + 1] % POINTS == wide % POINTS) & same) for t in range(modules)]
    other = dot(jnp.concatenate(picks, axis=0), form, EXACT)
    out = []
    for t in range(modules):
        theirs = other[t * rows : (t + 1) * rows]
        out.append(
            jnp.where(lane // 6 == t, form, 0.0)
            - jnp.where(lane // 6 == partner[:, t : t + 1] // POINTS, theirs, 0.0)
        )
    return jnp.concatenate(out, axis=0)


def coded(value, top):
    scale = jnp.where(top > 1e-30, TOP / jnp.maximum(top, 1e-30), 0.0)
    return jnp.round(value * scale).astype(jnp.int32).astype(jnp.int16)


def decoded(code, top):
    return code.astype(jnp.int32).astype(jnp.float32) * (top * (1.0 / TOP))


def largest(value):
    flat = value.reshape(-1, value.shape[-1])
    return jnp.max(jnp.abs(flat), axis=0, keepdims=True)


def steps_kernel(
    n_row, n_col, lags, groups,
    kernel_hbm, history_hbm, x_hbm, v_hbm, a_hbm, exc_hbm, solve_hbm, stiff_hbm, owned_hbm, links_hbm, arms_hbm,
    v_out, deck_out,
    kern, hist, past_t, x, v, a, exc, solve, stiff, owned, links, arms,
    k_t, acc, base_force, own_force, newest, window, pair_out, pair_in, line_out, line_in, outgoing, arrived,
    gaps, weights, base_out, predicted_last, pair_top_out, pair_top_in, line_top_out, line_top_in,
    local_sem, ag_send, ag_recv, pair_send, pair_recv, line_send, line_recv, top_send, top_recv, ex_send, ex_recv,
):
    row, col = lax.axis_index("row"), lax.axis_index("col")
    slab, reals = v.shape
    modules = slab // 6
    depth = n_row * slab
    block = n_col * slab
    half = block // PAIR
    wide = reals // PARTS
    n_line = n_col // PAIR
    grid_index = row * n_col + col
    line, side = col // PAIR, lax.rem(col, PAIR)
    other = 1 - side
    partner = line * PAIR + other

    sems = iter(range(64))

    def fetch(src, dst):
        copy = pltpu.make_async_copy(src, dst, local_sem.at[next(sems)])
        copy.start()
        return copy

    get_v = fetch(v_hbm, v)
    get_first = fetch(kernel_hbm.at[pl.ds(0, 1)], kern.at[pl.ds(0, 1)])
    get_groups = []
    for first, last in groups:
        get_groups.append(
            (
                fetch(history_hbm.at[pl.ds(first - 1, last - first)], hist.at[pl.ds(first - 1, last - first)]),
                fetch(kernel_hbm.at[pl.ds(first, last - first)], kern.at[pl.ds(first, last - first)]),
            )
        )
    ring, turn = row % ROW_RING, row // ROW_RING
    row_peers = [
        lax.rem(turn + t, n_row // ROW_RING) * ROW_RING + lax.rem(ring + d, ROW_RING)
        for t in (1, 0)
        for d in (2, 1, 3, 0)
        if t or d
    ]
    far_first = sorted(range(1, n_line), key=lambda d: -min(d, n_line - d))
    line_peers = [lax.rem(line + d, n_line) for d in far_first]

    barrier = pltpu.get_barrier_semaphore()
    for peer in row_peers:
        pl.semaphore_signal(barrier, inc=1, device_id={"row": peer}, device_id_type=MESH)
    pl.semaphore_signal(barrier, inc=1, device_id={"col": partner}, device_id_type=MESH)
    for peer in line_peers:
        pl.semaphore_signal(barrier, inc=1, device_id={"col": peer * PAIR + side}, device_id_type=MESH)
    pl.semaphore_wait(barrier, n_row - 1 + 1 + n_line - 1)

    def gather_copy(step, part, peer, source):
        return pltpu.make_async_remote_copy(
            src_ref=newest.at[step, part],
            dst_ref=window.at[step, part, source],
            send_sem=ag_send.at[step, part, peer],
            recv_sem=ag_recv.at[step, part, source],
            device_id={"row": peer},
            device_id_type=MESH,
        )

    def start_gather(step, part, value):
        newest[step, part] = value
        for peer in row_peers:
            gather_copy(step, part, peer, row).start()
        window[step, part, row] = value

    def wait_gather(step, part):
        for peer in row_peers:
            gather_copy(step, part, peer, peer).wait_recv()

    def pair_copy(step, part, piece):
        return pltpu.make_async_remote_copy(
            src_ref=pair_out.at[step, part, piece],
            dst_ref=pair_in.at[step, part, piece],
            send_sem=pair_send.at[step, part, piece],
            recv_sem=pair_recv.at[step, part, piece],
            device_id={"col": partner},
            device_id_type=MESH,
        )

    def pair_top_copy(step, part):
        return pltpu.make_async_remote_copy(
            src_ref=pair_top_out.at[step, part],
            dst_ref=pair_top_in.at[step, part],
            send_sem=top_send.at[step, part, n_line],
            recv_sem=top_recv.at[step, part, n_line],
            device_id={"col": partner},
            device_id_type=MESH,
        )

    def line_copy(step, part, peer, source):
        return pltpu.make_async_remote_copy(
            src_ref=line_out.at[step, part, peer],
            dst_ref=line_in.at[step, part, source],
            send_sem=line_send.at[step, part, peer],
            recv_sem=line_recv.at[step, part, source],
            device_id={"col": peer * PAIR + side},
            device_id_type=MESH,
        )

    def line_top_copy(step, part, peer, source):
        return pltpu.make_async_remote_copy(
            src_ref=line_top_out.at[step, part],
            dst_ref=line_top_in.at[step, part, source],
            send_sem=top_send.at[step, part, peer],
            recv_sem=top_recv.at[step, part, source],
            device_id={"col": peer * PAIR + side},
            device_id_type=MESH,
        )

    def exchange_copy(part, peer, source):
        return pltpu.make_async_remote_copy(
            src_ref=outgoing.at[part, peer],
            dst_ref=arrived.at[part, source],
            send_sem=ex_send.at[part, peer],
            recv_sem=ex_recv.at[part, source],
            device_id={"row": peer},
            device_id_type=MESH,
        )

    def window_of(step, part):
        return window[step, part].reshape(depth, wide)

    lanes = [slice(part * wide, (part + 1) * wide) for part in range(PARTS)]

    def lag_share(step, first, last):
        low = (first + 1 - step) * depth
        high = (last + 1 - step) * depth
        lag_block = kern[first:last].reshape((last - first) * depth, block)
        return dot(past_t[:, low:high], lag_block)

    def add_lags(step, index, fresh):
        share = lag_share(step, *groups[index])
        if fresh:
            acc[...] = share
        else:
            acc[...] += share

    def close_lags(step):
        base_force[step] = acc[...].T.reshape(n_line, PAIR, slab, reals)

    get_v.wait()
    for part in range(PARTS):
        start_gather(0, part, v[:, lanes[part]].astype(jnp.bfloat16))
    get_state = [fetch(x_hbm, x), fetch(a_hbm, a), fetch(exc_hbm, exc), fetch(solve_hbm, solve), fetch(stiff_hbm, stiff)]
    get_tables = [fetch(owned_hbm, owned), fetch(links_hbm, links), fetch(arms_hbm, arms)]
    get_first.wait()
    k_t[...] = kern[0].reshape(depth, block).T.reshape(n_line, PAIR, slab, depth)
    for index, (first, last) in enumerate(groups):
        for copy in get_groups[index]:
            copy.wait()
        for k in range(first - 1, last - 1):
            past_t[:, (k + 2) * depth : (k + 3) * depth] = hist[k].reshape(depth, reals).T
        add_lags(0, index, index == 0)
    close_lags(0)

    def half_force(step, part, which):
        now = dot(k_t[:, which].reshape(half, depth), window_of(step, part))
        return base_force[step, :, which][:, :, lanes[part]] + now.reshape(n_line, slab, wide)

    def send_force(step, part):
        wait_gather(step, part)
        theirs = half_force(step, part, other)
        top = largest(theirs)
        pair_top_out[step, part] = top
        pair_top_copy(step, part).start()
        own_force[part] = theirs
        for piece in [*line_peers, line]:
            pair_out[step, part, piece] = coded(own_force[part, piece], top)
            pair_copy(step, part, piece).start()
        mine = half_force(step, part, side)
        own_force[part] = mine
        return largest(mine)

    def pass_on(step, part, own_top):
        pair_top_copy(step, part).wait_recv()
        top_in = pair_top_in[step, part]
        top = own_top + top_in
        line_top_out[step, part] = top
        for peer in line_peers:
            pair_copy(step, part, peer).wait_recv()
            share = decoded(pair_in[step, part, peer], top_in)
            line_out[step, part, peer] = coded(own_force[part, peer] + share, top)
            line_copy(step, part, peer, line).start()
            line_top_copy(step, part, peer, line).start()
        pair_copy(step, part, line).wait_recv()
        own_force[part, line] = own_force[part, line] + decoded(pair_in[step, part, line], top_in)

    def collect(step, part):
        total = own_force[part, line]
        for peer in line_peers:
            line_top_copy(step, part, peer, peer).wait_recv()
            line_copy(step, part, peer, peer).wait_recv()
            total = total + decoded(line_in[step, part, peer], line_top_in[step, part, peer])
        return total

    own_top = [send_force(0, part) for part in range(PARTS)]

    for copy in get_state:
        copy.wait()
    solve_full = block_diagonal(solve, modules)
    solve_left = left_pieces(solve_full)
    stiff_left = left_pieces(block_diagonal(stiff, modules))

    def newest_past(step):
        for part in range(PARTS):
            past_t[lanes[part], (1 - step) * depth : (2 - step) * depth] = window_of(step, part).T

    def tables():
        for copy in get_tables:
            copy.wait()
        route = routing_matrix(owned[...], grid_index * modules, modules).astype(jnp.bfloat16)
        start = predicted_last[...]
        base_out[...] = dot(jnp.concatenate([route, route, route], axis=1), jnp.concatenate(pieces(start, 3), axis=0))
        weights[...] = left_pieces(dot(route.astype(jnp.float32), solve_full, EXACT))
        forms = dot(
            gap_matrix(links, arms, grid_index * modules * POINTS, modules),
            choice_matrix(owned[...], row, col, n_col * modules, modules),
            EXACT,
        )
        gaps[...] = left_pieces(forms)

    def fill_lags(step):
        order = [*range(1, len(groups)), 0]
        return [functools.partial(add_lags, step, index, i == 0) for i, index in enumerate(order)] + [
            functools.partial(close_lags, step)
        ]

    fillers = [fill_lags(1), fill_lags(2), [tables]]
    early_ends, late_ends = (0, 1, 0), (2, 3, 1)


    displacement, velocity, acceleration = x[...], v[...], a[...]
    for step in range(STEPS):
        predicted = displacement + DT * velocity + QUARTER * acceleration
        known = dot(solve_left, right_pieces(exc[step] - dot(stiff_left, right_pieces(predicted))))
        drift = velocity + 0.5 * DT * (acceleration + known)
        if step + 1 == STEPS:
            predicted_last[...] = predicted + QUARTER * known
        if step + 1 < STEPS:
            newest_past(step)
        work = fillers[step]
        for filler in work[: early_ends[step]]:
            filler()
        for part in range(PARTS):
            pass_on(step, part, own_top[part])
        for filler in work[early_ends[step] : late_ends[step]]:
            filler()
        answers = []
        for part in range(PARTS):
            total = right_pieces(collect(step, part))
            if step + 1 == STEPS:
                leaving = base_out[:, lanes[part]] - QUARTER * dot(weights[...], total)
                outgoing[part] = leaving.reshape(n_row, LANE_ROWS, wide)
                for peer in row_peers:
                    exchange_copy(part, peer, row).start()
                arrived[part, row] = outgoing[part, row]
                v_out[:, lanes[part]] = drift[:, lanes[part]] - 0.5 * DT * dot(solve_left, total)
            else:
                answers.append(dot(solve_left, total))
                newer = drift[:, lanes[part]] - 0.5 * DT * answers[part]
                start_gather(step + 1, part, newer.astype(jnp.bfloat16))
        if step + 1 < STEPS:
            answer = jnp.concatenate(answers, axis=1)
            velocity = drift - 0.5 * DT * answer
            acceleration = known - answer
            displacement = predicted + QUARTER * acceleration
            for filler in work[late_ends[step] :]:
                filler()
            own_top = [send_force(step + 1, part) for part in range(PARTS)]

    for part in range(PARTS):
        for step in range(STEPS):
            for peer in row_peers:
                gather_copy(step, part, peer, row).wait_send()
            pair_top_copy(step, part).wait_send()
            for piece in [*line_peers, line]:
                pair_copy(step, part, piece).wait_send()
            for peer in line_peers:
                line_top_copy(step, part, peer, line).wait_send()
                line_copy(step, part, peer, line).wait_send()
    for part in range(PARTS):
        for peer in row_peers:
            exchange_copy(part, peer, peer).wait_recv()
        everything = right_pieces(arrived[part].reshape(n_row * LANE_ROWS, wide))
        deck_out[:, lanes[part]] = dot(gaps[...], everything)
    for part in range(PARTS):
        for peer in row_peers:
            exchange_copy(part, peer, row).wait_send()


def body(
    n_row, n_col,
    kernel, history, displacement, velocity, acceleration, excitation, solve_inverse, stiffness, owned, links, arms,
):
    lags = kernel.shape[0]
    slab, reals = velocity.shape
    modules = slab // 6
    block = kernel.shape[3]
    depth = n_row * slab
    n_line = n_col // PAIR
    wide = reals // PARTS
    points = modules * POINTS * 3
    arrivals = n_row * LANE_ROWS
    anywhere = pl.BlockSpec(memory_space=pl.ANY)
    in_vmem = pl.BlockSpec(memory_space=pltpu.VMEM)
    groups = [(1, 2)] + [(k, min(k + 4, lags)) for k in range(2, lags, 4)]
    bf16, fp32, i32, i16 = jnp.bfloat16, jnp.float32, jnp.int32, jnp.int16
    vm = pltpu.VMEM
    sems = pltpu.SemaphoreType.DMA
    owned = owned.reshape(n_row, n_col * modules)
    solve_inverse = solve_inverse.transpose(1, 0, 2)
    stiffness = stiffness.transpose(1, 0, 2)
    arms = arms.transpose(1, 0, 2)
    v_last, gaps = pl.pallas_call(
        functools.partial(steps_kernel, n_row, n_col, lags, groups),
        out_shape=(vm((slab, reals), fp32), vm((points, reals), fp32)),
        in_specs=[anywhere] * 11,
        out_specs=(in_vmem, in_vmem),
        scratch_shapes=[
            vm(kernel.shape, bf16),
            vm(history.shape, bf16),
            vm((reals, (lags + 1) * depth), bf16),
            vm((slab, reals), fp32),
            vm((slab, reals), fp32),
            vm((slab, reals), fp32),
            vm(excitation.shape, fp32),
            vm(solve_inverse.shape, fp32),
            vm(stiffness.shape, fp32),
            vm(owned.shape, i32),
            vm(links.shape, i32),
            vm(arms.shape, fp32),
            vm((n_line, PAIR, slab, depth), bf16),
            vm((reals, block), fp32),
            vm((STEPS, n_line, PAIR, slab, reals), fp32),
            vm((PARTS, n_line, slab, wide), fp32),
            vm((STEPS, PARTS, slab, wide), bf16),
            vm((STEPS, PARTS, n_row, slab, wide), bf16),
            vm((STEPS, PARTS, n_line, slab, wide), i16),
            vm((STEPS, PARTS, n_line, slab, wide), i16),
            vm((STEPS, PARTS, n_line, slab, wide), i16),
            vm((STEPS, PARTS, n_line, slab, wide), i16),
            vm((PARTS, n_row, LANE_ROWS, wide), fp32),
            vm((PARTS, n_row, LANE_ROWS, wide), fp32),
            vm((points, 4 * arrivals), bf16),
            vm((arrivals, 4 * slab), bf16),
            vm((arrivals, reals), fp32),
            vm((slab, reals), fp32),
            vm((STEPS, PARTS, 1, wide), fp32),
            vm((STEPS, PARTS, 1, wide), fp32),
            vm((STEPS, PARTS, 1, wide), fp32),
            vm((STEPS, PARTS, n_line, 1, wide), fp32),
            sems((32,)),
            sems((STEPS, PARTS, n_row)),
            sems((STEPS, PARTS, n_row)),
            sems((STEPS, PARTS, n_line)),
            sems((STEPS, PARTS, n_line)),
            sems((STEPS, PARTS, n_line)),
            sems((STEPS, PARTS, n_line)),
            sems((STEPS, PARTS, n_line + 1)),
            sems((STEPS, PARTS, n_line + 1)),
            sems((PARTS, n_row)),
            sems((PARTS, n_row)),
        ],
        compiler_params=pltpu.CompilerParams(
            collective_id=0, has_side_effects=True, vmem_limit_bytes=56 * 1024 * 1024
        ),
    )(kernel, history, displacement, velocity, acceleration, excitation, solve_inverse, stiffness, owned, links, arms)
    return v_last, gaps.reshape(modules, 3, POINTS, reals).transpose(0, 2, 1, 3)


def solution(mesh):
    placed = (
        P(None, None, "col", "row"),
        P(None, None, "col", "sea"),
        P(("row", "col"), "sea"),
        P(("row", "col"), "sea"),
        P(("row", "col"), "sea"),
        P(None, ("row", "col"), "sea"),
        P(("row", "col"), None, None),
        P(("row", "col"), None, None),
        P(),
        P(("row", "col"), None),
        P(("row", "col"), None, None),
    )
    return jax.shard_map(
        functools.partial(body, mesh.shape["row"], mesh.shape["col"]),
        mesh=mesh,
        in_specs=placed,
        out_specs=(P(("row", "col"), "sea"), P(("row", "col"), None, None, "sea")),
        check_vma=False,
    )
```

```python
import functools

import jax
import jax.numpy as jnp
from jax import lax
from jax.experimental import pallas as pl
from jax.experimental.pallas import tpu as pltpu
from jax.sharding import PartitionSpec as P

POINTS = 16
STEPS = 3
SLOTS = 2
LANE_ROWS = 16

DT = 0.5
QUARTER = DT * DT / 4.0
TOP = 32000.0
PAIR = 2
ROW_RING = 4
PARTS = 2
MESH = pl.DeviceIdType.MESH
EXACT = lax.Precision.HIGHEST


def iota(shape, dim):
    return lax.broadcasted_iota(jnp.int32, shape, dim)


def f32(mask):
    return jnp.where(mask, 1.0, 0.0).astype(jnp.float32)


def dot(a, b, precision=None):
    return lax.dot_general(
        a, b, (((1,), (0,)), ((), ())), precision=precision, preferred_element_type=jnp.float32
    )


def dot_nt(a, b, precision=None):
    return lax.dot_general(
        a, b, (((1,), (1,)), ((), ())), precision=precision, preferred_element_type=jnp.float32
    )


def pieces(value, count):
    out = []
    for _ in range(count):
        out.append(value.astype(jnp.bfloat16))
        value = value - out[-1].astype(jnp.float32)
    return out


def left_pieces(matrix):
    high, low = pieces(matrix, 2)
    return jnp.concatenate([high, high, low, low], axis=1)


def right_pieces(matrix):
    high, low = pieces(matrix, 2)
    return jnp.concatenate([high, low, high, low], axis=0)


def block_diagonal(ref, modules):
    size = 6 * modules
    column = iota((size, size), 1)
    repeat = f32(iota((6, size), 1) % 6 == iota((6, size), 0))
    by_row = dot(ref[...].reshape(size, 6), repeat, EXACT)
    by_row = jnp.where(column // 6 == iota((size, size), 0) % modules, by_row, 0.0)
    order = f32(column == iota((size, size), 0) % 6 * modules + iota((size, size), 0) // 6)
    return dot(order, by_row, EXACT)


def routing_matrix(owned, base, modules):
    n_row, lanes = owned.shape
    lane = iota((n_row, lanes), 1)
    column = iota((n_row, modules), 1)
    out_rows = n_row * LANE_ROWS
    spread = f32(iota((modules, 6 * modules), 1) // 6 == iota((modules, 6 * modules), 0))
    total = jnp.zeros((out_rows, 6 * modules), jnp.float32)
    for slot in range(SLOTS):
        hit = jnp.zeros((n_row, modules), jnp.float32)
        for m in range(modules):
            here = f32((owned == base + m) & (lane % SLOTS == slot))
            hit = jnp.where(column == m, jnp.sum(here, axis=1, keepdims=True), hit)
        r = iota((out_rows, n_row), 0)
        lift = f32(
            (r // LANE_ROWS == iota((out_rows, n_row), 1))
            & (r % LANE_ROWS >= 6 * slot)
            & (r % LANE_ROWS < 6 * slot + 6)
        )
        wide = dot(dot(lift, hit), spread)
        rr = iota((out_rows, 6 * modules), 0) % LANE_ROWS - 6 * slot
        total = total + jnp.where(rr == iota((out_rows, 6 * modules), 1) % 6, wide, 0.0)
    return total


def choice_matrix(owned, row, col, home_size, modules):
    n_row, lanes = owned.shape
    home = owned // home_size
    mine = jnp.sum(jnp.where(iota((n_row, lanes), 0) == row, home, 0), axis=0, keepdims=True)
    per_lane = f32(iota((n_row, lanes), 0) == mine)
    size = 6 * modules
    pick = f32(iota((size, lanes), 1) == col * modules + iota((size, lanes), 0) // 6)
    by_row = dot_nt(pick, per_lane)
    out = n_row * LANE_ROWS
    widen = f32(iota((n_row, out), 1) // LANE_ROWS == iota((n_row, out), 0))
    wide = dot(by_row, widen)
    i = iota((size, out), 0)
    fits = iota((size, out), 1) % LANE_ROWS == 6 * (i // 6 % SLOTS) + i % 6
    return jnp.where(fits, wide, 0.0)


def gap_matrix(links_ref, arms_ref, first_point, modules):
    rows, size = 3 * POINTS, 6 * modules
    by_point = f32(iota((rows, POINTS), 0) % POINTS == iota((rows, POINTS), 1))
    levers = dot_nt(by_point, arms_ref[...].reshape(3 * modules, POINTS), EXACT)
    lane = iota((rows, size), 1)
    comp = iota((rows, size), 0) // POINTS
    mode = lane % 6
    spread = f32(iota((modules, size), 1) // 6 == iota((modules, size), 0))
    form = f32(mode == comp)
    for d in range(3):
        along = dot(levers[:, d * modules : (d + 1) * modules], spread, EXACT)
        form = form + jnp.where((mode == 3 + (comp + 1) % 3) & ((comp + 2) % 3 == d), along, 0.0)
        form = form - jnp.where((mode == 3 + (comp + 2) % 3) & ((comp + 1) % 3 == d), along, 0.0)
    local = (links_ref[...] - first_point).astype(jnp.float32)
    partner = dot_nt(by_point, local, EXACT).astype(jnp.int32)
    wide = iota((rows, rows), 1)
    same = wide // POINTS == iota((rows, rows), 0) // POINTS
    picks = [f32((partner[:, t : t + 1] % POINTS == wide % POINTS) & same) for t in range(modules)]
    other = dot(jnp.concatenate(picks, axis=0), form, EXACT)
    out = []
    for t in range(modules):
        theirs = other[t * rows : (t + 1) * rows]
        out.append(
            jnp.where(lane // 6 == t, form, 0.0)
            - jnp.where(lane // 6 == partner[:, t : t + 1] // POINTS, theirs, 0.0)
        )
    return jnp.concatenate(out, axis=0)


def coded(value, top):
    scale = jnp.where(top > 1e-30, TOP / jnp.maximum(top, 1e-30), 0.0)
    return jnp.round(value * scale).astype(jnp.int32).astype(jnp.int16)


def decoded(code, top):
    return code.astype(jnp.int32).astype(jnp.float32) * (top * (1.0 / TOP))


def largest(value):
    flat = value.reshape(-1, value.shape[-1])
    return jnp.max(jnp.abs(flat), axis=0, keepdims=True)


def steps_kernel(
    n_row, n_col, lags, groups,
    kernel_hbm, history_hbm, x_hbm, v_hbm, a_hbm, exc_hbm, solve_hbm, stiff_hbm, owned_hbm, links_hbm, arms_hbm,
    v_out, deck_out,
    kern, hist, past_t, x, v, a, exc, solve, stiff, owned, links, arms,
    k_t, acc, base_force, own_force, newest, window, pair_out, pair_in, line_out, line_in, outgoing, arrived,
    gaps, weights, base_out, predicted_last, pair_top_out, pair_top_in, line_top_out, line_top_in,
    local_sem, ag_send, ag_recv, pair_send, pair_recv, line_send, line_recv, top_send, top_recv, ex_send, ex_recv,
):
    row, col = lax.axis_index("row"), lax.axis_index("col")
    slab, reals = v.shape
    modules = slab // 6
    depth = n_row * slab
    block = n_col * slab
    half = block // PAIR
    wide = reals // PARTS
    n_line = n_col // PAIR
    grid_index = row * n_col + col
    line, side = col // PAIR, lax.rem(col, PAIR)
    other = 1 - side
    partner = line * PAIR + other

    sems = iter(range(64))

    def fetch(src, dst):
        copy = pltpu.make_async_copy(src, dst, local_sem.at[next(sems)])
        copy.start()
        return copy

    get_v = fetch(v_hbm, v)
    get_first = fetch(kernel_hbm.at[pl.ds(0, 1)], kern.at[pl.ds(0, 1)])
    get_groups = []
    for first, last in groups:
        get_groups.append(
            (
                fetch(history_hbm.at[pl.ds(first - 1, last - first)], hist.at[pl.ds(first - 1, last - first)]),
                fetch(kernel_hbm.at[pl.ds(first, last - first)], kern.at[pl.ds(first, last - first)]),
            )
        )
    ring, turn = row % ROW_RING, row // ROW_RING
    row_peers = [
        lax.rem(turn + t, n_row // ROW_RING) * ROW_RING + lax.rem(ring + d, ROW_RING)
        for t in (1, 0)
        for d in (2, 1, 3, 0)
        if t or d
    ]
    far_first = sorted(range(1, n_line), key=lambda d: (-min(d, n_line - d), -d))
    line_peers = [lax.rem(line + d, n_line) for d in far_first]

    barrier = pltpu.get_barrier_semaphore()
    for peer in row_peers:
        pl.semaphore_signal(barrier, inc=1, device_id={"row": peer}, device_id_type=MESH)
    pl.semaphore_signal(barrier, inc=1, device_id={"col": partner}, device_id_type=MESH)
    for peer in line_peers:
        pl.semaphore_signal(barrier, inc=1, device_id={"col": peer * PAIR + side}, device_id_type=MESH)
    pl.semaphore_wait(barrier, n_row - 1 + 1 + n_line - 1)

    def gather_copy(step, part, peer, source):
        return pltpu.make_async_remote_copy(
            src_ref=newest.at[step, part],
            dst_ref=window.at[step, part, source],
            send_sem=ag_send.at[step, part, peer],
            recv_sem=ag_recv.at[step, part, source],
            device_id={"row": peer},
            device_id_type=MESH,
        )

    def start_gather(step, part, value):
        newest[step, part] = value
        for peer in row_peers:
            gather_copy(step, part, peer, row).start()
        window[step, part, row] = value

    def wait_gather(step, part):
        for peer in row_peers:
            gather_copy(step, part, peer, peer).wait_recv()

    def pair_copy(step, part, piece):
        return pltpu.make_async_remote_copy(
            src_ref=pair_out.at[step, part, piece],
            dst_ref=pair_in.at[step, part, piece],
            send_sem=pair_send.at[step, part, piece],
            recv_sem=pair_recv.at[step, part, piece],
            device_id={"col": partner},
            device_id_type=MESH,
        )

    def pair_top_copy(step, part):
        return pltpu.make_async_remote_copy(
            src_ref=pair_top_out.at[step, part],
            dst_ref=pair_top_in.at[step, part],
            send_sem=top_send.at[step, part, n_line],
            recv_sem=top_recv.at[step, part, n_line],
            device_id={"col": partner},
            device_id_type=MESH,
        )

    def line_copy(step, part, peer, source):
        return pltpu.make_async_remote_copy(
            src_ref=line_out.at[step, part, peer],
            dst_ref=line_in.at[step, part, source],
            send_sem=line_send.at[step, part, peer],
            recv_sem=line_recv.at[step, part, source],
            device_id={"col": peer * PAIR + side},
            device_id_type=MESH,
        )

    def line_top_copy(step, part, peer, source):
        return pltpu.make_async_remote_copy(
            src_ref=line_top_out.at[step, part],
            dst_ref=line_top_in.at[step, part, source],
            send_sem=top_send.at[step, part, peer],
            recv_sem=top_recv.at[step, part, source],
            device_id={"col": peer * PAIR + side},
            device_id_type=MESH,
        )

    def exchange_copy(part, peer, source):
        return pltpu.make_async_remote_copy(
            src_ref=outgoing.at[part, peer],
            dst_ref=arrived.at[part, source],
            send_sem=ex_send.at[part, peer],
            recv_sem=ex_recv.at[part, source],
            device_id={"row": peer},
            device_id_type=MESH,
        )

    def window_of(step, part):
        return window[step, part].reshape(depth, wide)

    lanes = [slice(part * wide, (part + 1) * wide) for part in range(PARTS)]

    def lag_share(step, first, last):
        low = (first + 1 - step) * depth
        high = (last + 1 - step) * depth
        lag_block = kern[first:last].reshape((last - first) * depth, block)
        return dot(past_t[:, low:high], lag_block)

    def add_lags(step, index, fresh):
        share = lag_share(step, *groups[index])
        if fresh:
            acc[...] = share
        else:
            acc[...] += share

    def close_lags(step):
        base_force[step] = acc[...].T.reshape(n_line, PAIR, slab, reals)

    get_v.wait()
    for part in range(PARTS):
        start_gather(0, part, v[:, lanes[part]].astype(jnp.bfloat16))
    get_state = [fetch(x_hbm, x), fetch(a_hbm, a), fetch(exc_hbm, exc), fetch(solve_hbm, solve), fetch(stiff_hbm, stiff)]
    get_tables = [fetch(owned_hbm, owned), fetch(links_hbm, links), fetch(arms_hbm, arms)]
    get_first.wait()
    k_t[...] = kern[0].reshape(depth, block).T.reshape(n_line, PAIR, slab, depth)
    for index, (first, last) in enumerate(groups):
        for copy in get_groups[index]:
            copy.wait()
        for k in range(first - 1, last - 1):
            past_t[:, (k + 2) * depth : (k + 3) * depth] = hist[k].reshape(depth, reals).T
        add_lags(0, index, index == 0)
    close_lags(0)

    def half_force(step, part, which):
        now = dot(k_t[:, which].reshape(half, depth), window_of(step, part))
        return base_force[step, :, which][:, :, lanes[part]] + now.reshape(n_line, slab, wide)

    def send_force(step, part):
        wait_gather(step, part)
        theirs = half_force(step, part, other)
        top = largest(theirs)
        pair_top_out[step, part] = top
        pair_top_copy(step, part).start()
        own_force[part] = theirs
        for piece in [*line_peers, line]:
            pair_out[step, part, piece] = coded(own_force[part, piece], top)
            pair_copy(step, part, piece).start()
        mine = half_force(step, part, side)
        own_force[part] = mine
        return largest(mine)

    def pass_on(step, part, own_top):
        pair_top_copy(step, part).wait_recv()
        top_in = pair_top_in[step, part]
        top = own_top + top_in
        line_top_out[step, part] = top
        for peer in line_peers:
            pair_copy(step, part, peer).wait_recv()
            share = decoded(pair_in[step, part, peer], top_in)
            line_out[step, part, peer] = coded(own_force[part, peer] + share, top)
            line_copy(step, part, peer, line).start()
            line_top_copy(step, part, peer, line).start()
        pair_copy(step, part, line).wait_recv()
        own_force[part, line] = own_force[part, line] + decoded(pair_in[step, part, line], top_in)

    def collect(step, part):
        total = own_force[part, line]
        for peer in line_peers:
            line_top_copy(step, part, peer, peer).wait_recv()
            line_copy(step, part, peer, peer).wait_recv()
            total = total + decoded(line_in[step, part, peer], line_top_in[step, part, peer])
        return total

    own_top = [send_force(0, part) for part in range(PARTS)]

    def newest_past(step):
        for part in range(PARTS):
            past_t[lanes[part], (1 - step) * depth : (2 - step) * depth] = window_of(step, part).T

    def tables(solve_full):
        for copy in get_tables:
            copy.wait()
        route = routing_matrix(owned[...], grid_index * modules, modules).astype(jnp.bfloat16)
        start = predicted_last[...]
        base_out[...] = dot(jnp.concatenate([route, route, route], axis=1), jnp.concatenate(pieces(start, 3), axis=0))
        weights[...] = left_pieces(dot(route.astype(jnp.float32), solve_full, EXACT))
        forms = dot(
            gap_matrix(links, arms, grid_index * modules * POINTS, modules),
            choice_matrix(owned[...], row, col, n_col * modules, modules),
            EXACT,
        )
        gaps[...] = left_pieces(forms)

    def fill_lags(step):
        order = [*range(1, len(groups)), 0]
        return [functools.partial(add_lags, step, index, i == 0) for i, index in enumerate(order)] + [
            functools.partial(close_lags, step)
        ]

    fillers = [fill_lags(1), fill_lags(2), []]
    late_ends = (0, 0, 0)


    for step in range(STEPS):
        work = fillers[step]
        for part in range(PARTS):
            pass_on(step, part, own_top[part])
        if step == 0:
            for copy in get_state:
                copy.wait()
            solve_full = block_diagonal(solve, modules)
            solve_left = left_pieces(solve_full)
            stiff_left = left_pieces(block_diagonal(stiff, modules))
            displacement, velocity, acceleration = x[...], v[...], a[...]
        predicted = displacement + DT * velocity + QUARTER * acceleration
        known = dot(solve_left, right_pieces(exc[step] - dot(stiff_left, right_pieces(predicted))))
        drift = velocity + 0.5 * DT * (acceleration + known)
        if step + 1 == STEPS:
            predicted_last[...] = predicted + QUARTER * known
            tables(solve_full)
        for filler in work[: late_ends[step]]:
            filler()
        answers = []
        for part in range(PARTS):
            total = right_pieces(collect(step, part))
            if step + 1 == STEPS:
                leaving = base_out[:, lanes[part]] - QUARTER * dot(weights[...], total)
                outgoing[part] = leaving.reshape(n_row, LANE_ROWS, wide)
                for peer in row_peers:
                    exchange_copy(part, peer, row).start()
                arrived[part, row] = outgoing[part, row]
                v_out[:, lanes[part]] = drift[:, lanes[part]] - 0.5 * DT * dot(solve_left, total)
            else:
                answers.append(dot(solve_left, total))
                newer = drift[:, lanes[part]] - 0.5 * DT * answers[part]
                start_gather(step + 1, part, newer.astype(jnp.bfloat16))
        if step + 1 < STEPS:
            answer = jnp.concatenate(answers, axis=1)
            velocity = drift - 0.5 * DT * answer
            acceleration = known - answer
            displacement = predicted + QUARTER * acceleration
            newest_past(step)
            for filler in work[late_ends[step] :]:
                filler()
            own_top = [send_force(step + 1, part) for part in range(PARTS)]

    for part in range(PARTS):
        for step in range(STEPS):
            for peer in row_peers:
                gather_copy(step, part, peer, row).wait_send()
            pair_top_copy(step, part).wait_send()
            for piece in [*line_peers, line]:
                pair_copy(step, part, piece).wait_send()
            for peer in line_peers:
                line_top_copy(step, part, peer, line).wait_send()
                line_copy(step, part, peer, line).wait_send()
    for part in range(PARTS):
        for peer in row_peers:
            exchange_copy(part, peer, peer).wait_recv()
        everything = right_pieces(arrived[part].reshape(n_row * LANE_ROWS, wide))
        deck_out[:, lanes[part]] = dot(gaps[...], everything)
    for part in range(PARTS):
        for peer in row_peers:
            exchange_copy(part, peer, row).wait_send()


def body(
    n_row, n_col,
    kernel, history, displacement, velocity, acceleration, excitation, solve_inverse, stiffness, owned, links, arms,
):
    lags = kernel.shape[0]
    slab, reals = velocity.shape
    modules = slab // 6
    block = kernel.shape[3]
    depth = n_row * slab
    n_line = n_col // PAIR
    wide = reals // PARTS
    points = modules * POINTS * 3
    arrivals = n_row * LANE_ROWS
    anywhere = pl.BlockSpec(memory_space=pl.ANY)
    in_vmem = pl.BlockSpec(memory_space=pltpu.VMEM)
    groups = [(1, 2)] + [(k, min(k + 4, lags)) for k in range(2, lags, 4)]
    bf16, fp32, i32, i16 = jnp.bfloat16, jnp.float32, jnp.int32, jnp.int16
    vm = pltpu.VMEM
    sems = pltpu.SemaphoreType.DMA
    owned = owned.reshape(n_row, n_col * modules)
    solve_inverse = solve_inverse.transpose(1, 0, 2)
    stiffness = stiffness.transpose(1, 0, 2)
    arms = arms.transpose(1, 0, 2)
    v_last, gaps = pl.pallas_call(
        functools.partial(steps_kernel, n_row, n_col, lags, groups),
        out_shape=(vm((slab, reals), fp32), vm((points, reals), fp32)),
        in_specs=[anywhere] * 11,
        out_specs=(in_vmem, in_vmem),
        scratch_shapes=[
            vm(kernel.shape, bf16),
            vm(history.shape, bf16),
            vm((reals, (lags + 1) * depth), bf16),
            vm((slab, reals), fp32),
            vm((slab, reals), fp32),
            vm((slab, reals), fp32),
            vm(excitation.shape, fp32),
            vm(solve_inverse.shape, fp32),
            vm(stiffness.shape, fp32),
            vm(owned.shape, i32),
            vm(links.shape, i32),
            vm(arms.shape, fp32),
            vm((n_line, PAIR, slab, depth), bf16),
            vm((reals, block), fp32),
            vm((STEPS, n_line, PAIR, slab, reals), fp32),
            vm((PARTS, n_line, slab, wide), fp32),
            vm((STEPS, PARTS, slab, wide), bf16),
            vm((STEPS, PARTS, n_row, slab, wide), bf16),
            vm((STEPS, PARTS, n_line, slab, wide), i16),
            vm((STEPS, PARTS, n_line, slab, wide), i16),
            vm((STEPS, PARTS, n_line, slab, wide), i16),
            vm((STEPS, PARTS, n_line, slab, wide), i16),
            vm((PARTS, n_row, LANE_ROWS, wide), fp32),
            vm((PARTS, n_row, LANE_ROWS, wide), fp32),
            vm((points, 4 * arrivals), bf16),
            vm((arrivals, 4 * slab), bf16),
            vm((arrivals, reals), fp32),
            vm((slab, reals), fp32),
            vm((STEPS, PARTS, 1, wide), fp32),
            vm((STEPS, PARTS, 1, wide), fp32),
            vm((STEPS, PARTS, 1, wide), fp32),
            vm((STEPS, PARTS, n_line, 1, wide), fp32),
            sems((32,)),
            sems((STEPS, PARTS, n_row)),
            sems((STEPS, PARTS, n_row)),
            sems((STEPS, PARTS, n_line)),
            sems((STEPS, PARTS, n_line)),
            sems((STEPS, PARTS, n_line)),
            sems((STEPS, PARTS, n_line)),
            sems((STEPS, PARTS, n_line + 1)),
            sems((STEPS, PARTS, n_line + 1)),
            sems((PARTS, n_row)),
            sems((PARTS, n_row)),
        ],
        compiler_params=pltpu.CompilerParams(
            collective_id=0, has_side_effects=True, vmem_limit_bytes=56 * 1024 * 1024
        ),
    )(kernel, history, displacement, velocity, acceleration, excitation, solve_inverse, stiffness, owned, links, arms)
    return v_last, gaps.reshape(modules, 3, POINTS, reals).transpose(0, 2, 1, 3)


def solution(mesh):
    placed = (
        P(None, None, "col", "row"),
        P(None, None, "col", "sea"),
        P(("row", "col"), "sea"),
        P(("row", "col"), "sea"),
        P(("row", "col"), "sea"),
        P(None, ("row", "col"), "sea"),
        P(("row", "col"), None, None),
        P(("row", "col"), None, None),
        P(),
        P(("row", "col"), None),
        P(("row", "col"), None, None),
    )
    return jax.shard_map(
        functools.partial(body, mesh.shape["row"], mesh.shape["col"]),
        mesh=mesh,
        in_specs=placed,
        out_specs=(P(("row", "col"), "sea"), P(("row", "col"), None, None, "sea")),
        check_vma=False,
    )
```
